32 devices in a mesh: dp: 8 (over y, x, core), vocab: 4 (over z).
Axes of the slice: x: 2, y: 2, z: 4, core: 2. Of those that a mesh axis runs over, the one named last changes fastest.
Arguments:
- student_hidden: bfloat16 [192, 3584], P('dp'), may hold values from -110 to 110
- teacher_hidden: bfloat16 [192, 4608], P('dp'), may hold values from -110 to 110
- student_head: bfloat16 [3584, 16384], P(None, ('dp', 'vocab')), may hold values from -0.09375 to 0.09375
- teacher_head: bfloat16 [4608, 16384], P(None, ('dp', 'vocab')), may hold values from -0.09375 to 0.09375
- live_count: int32 [8], P('dp'), may hold values from 1 to 24, as said below
- teacher_count: int32 [8], P('dp'), may hold values from 1 to 24, as said below
- teacher_dest: int32 [192], P('dp'), may hold values from 0 to 191, as said below
Outputs:
- distill_loss: float32 [], replicated
- grad_hidden: bfloat16 [192, 3584], P('dp', 'vocab')
- grad_head: bfloat16 [3584, 16384], P(None, ('dp', 'vocab'))
The draws below stay inside these ranges and needn't reach their ends.
Inputs may be any that keep to these rules, and one draw needn't show every extreme that they name: Shard s's covered tokens are its first live_count[s] tokens; the counts sum to 96. Data shard j's filled teacher row slots are its first teacher_count[j] slots; the counts sum to 96. `teacher_dest`: A filled slot names the global index of a covered token; every covered token is named by exactly one filled slot. Unfilled slots hold arbitrary indices.
All inputs are finite; a program needn't handle non-finite values.
Results may differ from the reference program's by a relative error of at most 0.014.
Values may be sent and summed in bfloat16 or wider, within the bound.
A program may use at most 128 MiB of HBM per device.

```python
import jax
import jax.numpy as jnp
from jax import lax

DS = 3584
DT = 4608
TOK_DEV = 24
TOKENS = 192
LIVE = 96
VOCAB = 16384
N_DP = 8


def skewed_counts(key):
    half_rows = TOK_DEV // 2
    shuffled = jax.random.permutation(key, N_DP)
    remaining = N_DP - 3
    pair_count = remaining // 2
    pair_moves = jax.random.randint(jax.random.fold_in(key, 1), (pair_count,), 0, half_rows)
    paired = jnp.stack([pair_moves, -pair_moves], axis=1).reshape(-1)
    opening = jnp.array([half_rows, -(half_rows // 2), -(half_rows // 2)], jnp.int32)
    changes = jnp.concatenate([opening, paired.astype(jnp.int32), jnp.zeros((remaining - 2 * pair_count,), jnp.int32)])
    return half_rows + jnp.zeros((N_DP,), jnp.int32).at[shuffled].set(changes)


def routing_tables(key):
    live_counts = skewed_counts(jax.random.fold_in(key, 101))
    teacher_counts = skewed_counts(jax.random.fold_in(key, 102))
    position = lax.broadcasted_iota(jnp.int32, (N_DP, TOK_DEV), 1)
    row_flags = (position < live_counts[:, None]).reshape(-1).astype(jnp.int32)
    live_total = TOKENS // 2
    ordered = jnp.argsort(1 - row_flags, stable=True)[:live_total]
    listing = ordered[jax.random.permutation(jax.random.fold_in(key, 103), live_total)]
    offsets = jnp.cumsum(teacher_counts) - teacher_counts
    slot_index = offsets[:, None] + position
    slot_valid = position < teacher_counts[:, None]
    filler = jax.random.randint(jax.random.fold_in(key, 104), (N_DP, TOK_DEV), 0, TOKENS)
    destination = jnp.where(slot_valid, listing[jnp.clip(slot_index, 0, live_total - 1)], filler)
    return (live_counts, teacher_counts, destination.reshape(-1).astype(jnp.int32))


def draw_live_count(key, part):
    return routing_tables(key)[0]


def draw_teacher_count(key, part):
    return routing_tables(key)[1]


def draw_teacher_dest(key, part):
    return routing_tables(key)[2]


def draw_student_hidden(key, part):
    key = jax.random.fold_in(key, 5)
    values = 3.0 * jnp.clip(jax.random.normal(key, (TOKENS, DS), jnp.float32), -6.0, 6.0)
    return values.astype(jnp.bfloat16)


def draw_teacher_hidden(key, part):
    key = jax.random.fold_in(key, 6)
    values = 3.0 * jnp.clip(jax.random.normal(key, (TOKENS, DT), jnp.float32), -6.0, 6.0)
    return values.astype(jnp.bfloat16)


def block_levels(rng, dims, split, smallest, high):
    def one(dim, parts):
        draws = jax.random.uniform(jax.random.fold_in(jax.random.fold_in(rng, 6), dim), (parts,), jnp.float32, smallest / len(split), high / len(split))
        return jnp.repeat(jnp.exp(draws), dims[dim] // parts).reshape((-1,) + (1,) * (len(dims) - dim - 1))

    loudness = one(*split[0])
    for cut in split[1:]:
        loudness = loudness * one(*cut)
    return loudness


def gaussian(own_key, dims, deviation, most, split=(), dtype=jnp.bfloat16):
    values = jax.random.normal(own_key, dims, jnp.float32) * deviation
    if len(split) > 0:
        values = block_levels(own_key, dims, split, -0.22, 0.18) * values
    return jnp.clip(values, min=-most, max=most).astype(dtype)


def setup_inputs(seed: int = 0) -> dict:
    streams_of = jax.random.split(jax.random.key(seed), 8)
    return {
        "student_hidden": draw_student_hidden(jax.random.fold_in(streams_of[7], 71), 0),
        "teacher_hidden": draw_teacher_hidden(jax.random.fold_in(streams_of[7], 71), 0),
        "student_head": gaussian(streams_of[2], (DS, VOCAB), DS ** -0.5, 0.09375, ((1, 32),)),
        "teacher_head": gaussian(streams_of[3], (DT, VOCAB), DT ** -0.5, 0.09375, ((1, 32),)),
        "live_count": draw_live_count(jax.random.fold_in(streams_of[7], 71), 0),
        "teacher_count": draw_teacher_count(jax.random.fold_in(streams_of[7], 71), 0),
        "teacher_dest": draw_teacher_dest(jax.random.fold_in(streams_of[7], 71), 0),
    }


loss_scale = 65536.0


def reference(student_hidden, teacher_hidden, student_head, teacher_head, live_count, teacher_count, teacher_dest):
    position = lax.broadcasted_iota(jnp.int32, (N_DP, TOK_DEV), 1)
    live_flag = (position < live_count[:, None]).reshape(-1)
    slot_ok = (position < teacher_count[:, None]).reshape(-1)
    target = jnp.where(slot_ok, teacher_dest, TOKENS).astype(jnp.int32)
    aligned = jnp.zeros((TOKENS, DT), jnp.bfloat16).at[target].set(teacher_hidden, mode="drop")
    student_logits = jnp.dot(student_hidden, student_head, preferred_element_type=jnp.float32)
    teacher_logits = jnp.dot(aligned, teacher_head, preferred_element_type=jnp.float32)
    teacher_top = jnp.max(teacher_logits, axis=1)
    student_top = jnp.max(student_logits, axis=1)
    teacher_weights = jnp.exp(teacher_logits - teacher_top[:, None])
    teacher_sum = jnp.sum(teacher_weights, axis=1)
    student_sum = jnp.sum(jnp.exp(student_logits - student_top[:, None]), axis=1)
    cross_sum = jnp.sum(teacher_weights * (teacher_logits - student_logits), axis=1)
    teacher_norm = teacher_top + jnp.log(teacher_sum)
    student_norm = student_top + jnp.log(student_sum)
    divergence = cross_sum / teacher_sum - teacher_norm + student_norm
    distill_loss = jnp.sum(jnp.where(live_flag, divergence, 0.0)) / LIVE
    probs_gap = jnp.exp(student_logits - student_norm[:, None]) - jnp.exp(teacher_logits - teacher_norm[:, None])
    logit_grad = jnp.where(live_flag[:, None], probs_gap * (loss_scale / LIVE), 0.0).astype(jnp.bfloat16)
    grad_head = lax.dot_general(student_hidden, logit_grad, (((0,), (0,)), ((), ())), preferred_element_type=jnp.float32)
    grad_hidden = lax.dot_general(logit_grad, student_head, (((1,), (1,)), ((), ())), preferred_element_type=jnp.float32)
    return distill_loss, grad_hidden.astype(jnp.bfloat16), grad_head.astype(jnp.bfloat16)
```

```python
import functools

import jax
import jax.numpy as jnp
from jax import lax
from jax.experimental import pallas as pl
from jax.experimental.pallas import tpu as pltpu
from jax.sharding import PartitionSpec as P

loss_scale = 65536.0
MESH = pl.DeviceIdType.MESH


def nt(a, b):
    return lax.dot_general(a, b, (((1,), (1,)), ((), ())), preferred_element_type=jnp.float32)


def tn(a, b):
    return lax.dot_general(a, b, (((0,), (0,)), ((), ())), preferred_element_type=jnp.float32)


def nn(a, b):
    return jnp.dot(a, b, preferred_element_type=jnp.float32)


def merge(parts, count):
    t_top = parts[0, 0:1]
    s_top = parts[0, 1:2]
    for i in range(1, count):
        t_top = jnp.maximum(t_top, parts[i, 0:1])
        s_top = jnp.maximum(s_top, parts[i, 1:2])
    t_sum = jnp.zeros_like(t_top)
    s_sum = jnp.zeros_like(t_top)
    cross = jnp.zeros_like(t_top)
    for i in range(count):
        t_scale = jnp.exp(parts[i, 0:1] - t_top)
        t_sum += parts[i, 2:3] * t_scale
        cross += parts[i, 4:5] * t_scale
        s_sum += parts[i, 3:4] * jnp.exp(parts[i, 1:2] - s_top)
    return t_top, s_top, t_sum, s_sum, cross


def main_kernel(
    n, nv, rows, live, tiles,
    sh_ref, th_ref, meta_ref, shead_hbm, thead_hbm,
    loss_ref, hc_ref, lg_ref, gh_ref,
    gs, gt, gm, shead, thead, onehot_s, onehot_t, s_log, t_log,
    st, sz, lgx, core_out, core_in, mine, plane_out, plane_in, own, z_out, z_in,
    head_sem, m_send, m_recv, ici_send, core_send, g_recv,
    st_send, st_recv, sz_send, sz_recv, c_send, c_recv, p_send, p_recv, z_send, z_recv,
):
    nc = n // 2
    me = lax.axis_index("dp")
    vi = lax.axis_index("vocab")
    core = lax.rem(me, 2)
    chip = lax.div(me, 2)
    partner = 2 * chip + 1 - core
    pair = 2 * rows
    width = n * pair
    ds, dt = shead.shape[0], thead.shape[0]

    head_copies = [
        pltpu.make_async_copy(shead_hbm, shead, head_sem.at[0]),
        pltpu.make_async_copy(thead_hbm, thead, head_sem.at[1]),
    ]
    for copy in head_copies:
        copy.start()

    barrier = pltpu.get_barrier_semaphore()
    for r in range(1, n):
        pl.semaphore_signal(barrier, inc=1, device_id={"dp": lax.rem(me + r, n)}, device_id_type=MESH)
    for r in range(1, nv):
        pl.semaphore_signal(barrier, inc=1, device_id={"vocab": lax.rem(vi + r, nv)}, device_id_type=MESH)

    def folded(ref):
        half = ref.shape[1] // 2
        wide = ref[...].astype(jnp.float32)
        return jnp.concatenate([wide[:, :half], wide[:, half:]], axis=0).astype(jnp.bfloat16)

    gs[me] = folded(sh_ref)
    gt[me] = folded(th_ref)
    gm[me] = meta_ref[...]
    pl.semaphore_wait(barrier, n - 1 + nv - 1)

    def remote(src, dst, send, recv, target):
        return pltpu.make_async_remote_copy(
            src_ref=src, dst_ref=dst, send_sem=send, recv_sem=recv,
            device_id=target, device_id_type=MESH,
        )

    waits = []

    def go(copy):
        copy.start()
        waits.append(copy)

    for r in range(1, n):
        target = lax.rem(me + r, n)
        go(remote(gm.at[me], gm.at[me], m_send.at[r], m_recv.at[me], {"dp": target}))
    bufs = (gs, gt)
    for b, buf in enumerate(bufs):
        for r in range(1, nc):
            target = 2 * lax.rem(chip + r, nc) + core
            go(remote(buf.at[me], buf.at[me], ici_send.at[b, r], g_recv.at[b, me], {"dp": target}))
        go(remote(buf.at[me], buf.at[me], core_send.at[b, 0], g_recv.at[b, me], {"dp": partner}))

    def gather(b):
        buf = bufs[b]
        for r in range(1, nc):
            shard = 2 * lax.rem(chip + nc - r, nc) + core
            remote(buf.at[shard], buf.at[shard], core_send.at[b, r], g_recv.at[b, shard], {"dp": partner}).wait_recv()
            go(remote(buf.at[shard], buf.at[shard], core_send.at[b, r], g_recv.at[b, shard], {"dp": partner}))

    for r in range(1, n):
        shard = lax.rem(me + r, n)
        remote(gm.at[shard], gm.at[shard], m_send.at[r], m_recv.at[shard], {"dp": shard}).wait_recv()
    meta = gm[0]
    for i in range(1, n):
        meta = meta + gm[i]
    live_l, off_l, count_l, dest_l = meta[0:1], meta[1:2], meta[2:3], meta[3:4]

    lane = lax.broadcasted_iota(jnp.int32, (1, width), 1)
    half_l = jnp.zeros((1, width), jnp.int32)
    pos_l = lane
    for i in range(1, 2 * n):
        pos_l = jnp.where(lane >= i * rows, lane - i * rows, pos_l)
        if i % 2:
            half_l = jnp.where((lane >= i * rows) & (lane < (i + 1) * rows), 1, half_l)
    rank_l = jnp.zeros((1, width), jnp.int32)
    for i in range(n):
        off_i = off_l[:, i * pair:i * pair + 1]
        inside = (dest_l >= i * rows) & (dest_l < (i + 1) * rows)
        rank_l = jnp.where(inside, dest_l - i * rows + off_i, rank_l)
    shape = (2 * live, width)
    row = lax.broadcasted_iota(jnp.int32, shape, 0)
    key_s = jnp.where(pos_l < live_l, pos_l + off_l + live * half_l, -1)
    key_t = jnp.where(pos_l < count_l, rank_l + live * half_l, -1)
    onehot_s[...] = jnp.where(row == key_s, 1.0, 0.0).astype(jnp.bfloat16)
    onehot_t[...] = jnp.where(row == key_t, 1.0, 0.0).astype(jnp.bfloat16)

    def logits(b, onehot, head, out, keep, tile):
        buf = bufs[b]
        half = buf.shape[2]
        out[...] = jnp.zeros_like(out)

        def step(i, carry):
            at = pl.multiple_of(i * tile, 128)
            block = buf[:, :, pl.ds(at, tile)].reshape(width, tile)
            packed = nn(onehot[...], block).astype(jnp.bfloat16)
            top, low = packed[:live], packed[live:]
            if keep is not None:
                keep[:, pl.ds(at, tile)] = top
                keep[:, pl.ds(pl.multiple_of(half + at, 128), tile)] = low
            out[...] += nn(top, head[pl.ds(at, tile), :]) + nn(low, head[pl.ds(half + at, tile), :])
            return carry

        lax.fori_loop(0, half // tile, step, 0)

    def rest(b):
        buf = bufs[b]
        for r in range(nc):
            shard = 2 * lax.rem(chip + nc - r, nc) + 1 - core
            remote(buf.at[shard], buf.at[shard], core_send.at[b, r], g_recv.at[b, shard], {"dp": partner}).wait_recv()

    gather(0)
    rest(0)
    head_copies[0].wait()
    logits(0, onehot_s, shead, s_log, hc_ref, tiles[0])
    gather(1)
    rest(1)
    head_copies[1].wait()
    logits(1, onehot_t, thead, t_log, None, tiles[1])

    lanes = st.shape[2]
    s_val, t_val = s_log[...], t_log[...]
    t_top = jnp.max(t_val, axis=1, keepdims=True)
    s_top = jnp.max(s_val, axis=1, keepdims=True)
    t_exp = jnp.exp(t_val - t_top)
    t_sum = jnp.sum(t_exp, axis=1, keepdims=True)
    s_sum = jnp.sum(jnp.exp(s_val - s_top), axis=1, keepdims=True)
    cross = jnp.sum(t_exp * (t_val - s_val), axis=1, keepdims=True)
    col = lax.broadcasted_iota(jnp.int32, (live, 128), 1)
    table = jnp.where(col == 0, t_top, 1.0)
    for i, value in ((1, s_top), (2, t_sum), (3, s_sum), (4, cross)):
        table = jnp.where(col == i, value, table)
    if lanes > live:
        table = jnp.concatenate([table, jnp.ones((lanes - live, 128), jnp.float32)], axis=0)
    st[me] = jnp.transpose(table)[0:8]
    for r in range(1, n):
        go(remote(st.at[me], st.at[me], st_send.at[r], st_recv.at[me], {"dp": lax.rem(me + r, n)}))
    for r in range(1, n):
        shard = lax.rem(me + r, n)
        remote(st.at[shard], st.at[shard], st_send.at[r], st_recv.at[shard], {"dp": shard}).wait_recv()
    joined = merge(st, n)
    ones = jnp.ones((3, lanes), jnp.float32)
    sz[vi] = jnp.concatenate(list(joined) + [ones], axis=0)
    for r in range(1, nv):
        go(remote(sz.at[vi], sz.at[vi], sz_send.at[r], sz_recv.at[vi], {"vocab": lax.rem(vi + r, nv)}))
    for r in range(1, nv):
        shard = lax.rem(vi + r, nv)
        remote(sz.at[shard], sz.at[shard], sz_send.at[r], sz_recv.at[shard], {"vocab": shard}).wait_recv()
    t_top, s_top, t_sum, s_sum, cross = merge(sz, nv)
    t_norm = t_top + jnp.log(t_sum)
    s_norm = s_top + jnp.log(s_sum)
    divergence = cross / t_sum - t_norm + s_norm
    lane = lax.broadcasted_iota(jnp.int32, (1, lanes), 1)
    divergence = jnp.where(lane < live, divergence, 0.0)
    loss_ref[...] = jnp.sum(divergence, axis=1, keepdims=True) / live
    norms = jnp.concatenate([t_norm, s_norm, jnp.zeros((126, lanes), jnp.float32)], axis=0)
    norms = jnp.transpose(norms)[:live]
    gap = jnp.exp(s_val - norms[:, 1:2]) - jnp.exp(t_val - norms[:, 0:1])
    grad = (gap * (loss_scale / live)).astype(jnp.bfloat16)
    lg_ref[...] = grad

    spread = tn(onehot_s[0:live, :], grad)
    for k in range(2):
        lgx[k] = jnp.concatenate(
            [spread[(2 * c + k) * pair:(2 * c + k) * pair + rows] for c in range(nc)], axis=0
        ).astype(jnp.bfloat16)

    half = core_out.shape[3]

    def partial(k, v):
        base = pl.multiple_of(v * (2 * half), 16)
        low = nt(lgx[k], shead[pl.ds(base, half), :])
        high = nt(lgx[k], shead[pl.ds(pl.multiple_of(base + half, 16), half), :])
        return [
            jnp.concatenate([low[c * rows:(c + 1) * rows], high[c * rows:(c + 1) * rows]], axis=0)
            for c in range(nc)
        ]

    for j in range(nv):
        v = lax.rem(vi + 1 + j, nv)
        for c, block in enumerate(partial(1 - core, v)):
            core_out[j, c] = block.astype(jnp.bfloat16)
        go(remote(core_out.at[j], core_in.at[j], c_send.at[j], c_recv.at[j], {"dp": partner}))
        for c, block in enumerate(partial(core, v)):
            mine[j, c] = block
    for j in range(nv):
        remote(core_out.at[j], core_in.at[j], c_send.at[j], c_recv.at[j], {"dp": partner}).wait_recv()
        mine[j] = mine[j] + core_in[j].astype(jnp.float32)
        plane_out[j] = mine[j].astype(jnp.bfloat16)
        for r in range(1, nc):
            to = lax.rem(chip + r, nc)
            go(remote(plane_out.at[j, to], plane_in.at[j, r], p_send.at[j, r], p_recv.at[j, r], {"dp": 2 * to + core}))
    for j in range(nv):
        total = mine[j, chip]
        for r in range(1, nc):
            remote(plane_in.at[j, r], plane_in.at[j, r], p_send.at[j, r], p_recv.at[j, r], {"dp": partner}).wait_recv()
            total = total + plane_in[j, r].astype(jnp.float32)
        if j < nv - 1:
            z_out[j] = total.astype(jnp.bfloat16)
            go(remote(z_out.at[j], z_in.at[j], z_send.at[j], z_recv.at[j], {"vocab": lax.rem(vi + 1 + j, nv)}))
        else:
            own[...] = total
    total = own[...]
    for j in range(nv - 1):
        remote(z_in.at[j], z_in.at[j], z_send.at[j], z_recv.at[j], {"vocab": lax.rem(vi + 1, nv)}).wait_recv()
        total = total + z_in[j].astype(jnp.float32)
    gh_ref[...] = total.astype(jnp.bfloat16)
    for copy in waits:
        copy.wait_send()


def head_kernel(hc_ref, lg_ref, out_ref):
    out_ref[...] = tn(hc_ref[...], lg_ref[...]).astype(jnp.bfloat16)


def per_device(
    student_hidden,
    teacher_hidden,
    student_head,
    teacher_head,
    live_count,
    teacher_count,
    teacher_dest,
):
    rows, ds = student_hidden.shape
    dt = teacher_hidden.shape[1]
    vocab = student_head.shape[1]
    n = lax.axis_size("dp")
    nv = lax.axis_size("vocab")
    nc = n // 2
    live = rows * n // 2
    lanes = -(-live // 128) * 128
    pair = 2 * rows
    width = n * pair
    half = ds // nv // 2
    me = lax.axis_index("dp")

    lane_shard = lax.broadcasted_iota(jnp.int32, (width,), 0) // pair
    here = lane_shard == me
    dest = jnp.tile(teacher_dest, 2 * n)
    zero = jnp.zeros((width,), jnp.int32)
    meta = jnp.stack(
        [
            jnp.where(here, live_count[0], 0),
            jnp.where(lane_shard > me, live_count[0], 0),
            jnp.where(here, teacher_count[0], 0),
            jnp.where(here, dest, 0),
            zero, zero, zero, zero,
        ]
    )
    bf16, f32 = jnp.bfloat16, jnp.float32
    vmem = pl.BlockSpec(memory_space=pltpu.VMEM)
    hbm = pl.BlockSpec(memory_space=pl.ANY)
    dma = pltpu.SemaphoreType.DMA
    loss, hc, lg, gh = pl.pallas_call(
        functools.partial(main_kernel, n, nv, rows, live, (896, 768)),
        out_shape=(
            jax.ShapeDtypeStruct((1, 1), f32),
            jax.ShapeDtypeStruct((live, ds), bf16),
            jax.ShapeDtypeStruct((live, vocab), bf16),
            jax.ShapeDtypeStruct((pair, half), bf16),
        ),
        in_specs=[vmem, vmem, vmem, hbm, hbm],
        out_specs=(vmem, vmem, vmem, vmem),
        scratch_shapes=[
            pltpu.VMEM((n, pair, ds // 2), bf16),
            pltpu.VMEM((n, pair, dt // 2), bf16),
            pltpu.VMEM((n, 8, width), jnp.int32),
            pltpu.VMEM((ds, vocab), bf16),
            pltpu.VMEM((dt, vocab), bf16),
            pltpu.VMEM((2 * live, width), bf16),
            pltpu.VMEM((2 * live, width), bf16),
            pltpu.VMEM((live, vocab), f32),
            pltpu.VMEM((live, vocab), f32),
            pltpu.VMEM((n, 8, lanes), f32),
            pltpu.VMEM((nv, 8, lanes), f32),
            pltpu.VMEM((2, nc * rows, vocab), bf16),
            pltpu.VMEM((nv, nc, pair, half), bf16),
            pltpu.VMEM((nv, nc, pair, half), bf16),
            pltpu.VMEM((nv, nc, pair, half), f32),
            pltpu.VMEM((nv, nc, pair, half), bf16),
            pltpu.VMEM((nv, nc, pair, half), bf16),
            pltpu.VMEM((pair, half), f32),
            pltpu.VMEM((nv, pair, half), bf16),
            pltpu.VMEM((nv, pair, half), bf16),
            dma((2,)),
            dma((n,)), dma((n,)),
            dma((2, nc)), dma((2, nc)), dma((2, n)),
            dma((n,)), dma((n,)), dma((nv,)), dma((nv,)),
            dma((nv,)), dma((nv,)), dma((nv, nc)), dma((nv, nc)), dma((nv,)), dma((nv,)),
        ],
        compiler_params=pltpu.CompilerParams(
            collective_id=0, has_side_effects=True, vmem_limit_bytes=58 * 2**20
        ),
        name="distill",
    )(student_hidden, teacher_hidden, meta, student_head, teacher_head)
    tile = 512
    grad_head = pl.pallas_call(
        head_kernel,
        grid=(ds // tile,),
        out_shape=jax.ShapeDtypeStruct((ds, vocab), bf16),
        in_specs=[
            pl.BlockSpec((live, tile), lambda i: (0, i)),
            pl.BlockSpec((live, vocab), lambda i: (0, 0)),
        ],
        out_specs=pl.BlockSpec((tile, vocab), lambda i: (i, 0)),
        name="head_grad",
    )(hc, lg)
    grad_hidden = jnp.concatenate([gh[:rows], gh[rows:]], axis=1)
    return (loss[0, 0], grad_hidden, grad_head)


def solution(mesh):
    return jax.shard_map(
        per_device,
        mesh=mesh,
        in_specs=(
            P("dp", None),
            P("dp", None),
            P(None, ("dp", "vocab")),
            P(None, ("dp", "vocab")),
            P("dp"),
            P("dp"),
            P("dp"),
        ),
        out_specs=(P(), P("dp", "vocab"), P(None, ("dp", "vocab"))),
        check_vma=False,
    )
```

```python
import functools

import jax
import jax.numpy as jnp
from jax import lax
from jax.experimental import pallas as pl
from jax.experimental.pallas import tpu as pltpu
from jax.sharding import PartitionSpec as P

loss_scale = 65536.0
MESH = pl.DeviceIdType.MESH


def nt(a, b):
    return lax.dot_general(a, b, (((1,), (1,)), ((), ())), preferred_element_type=jnp.float32)


def tn(a, b):
    return lax.dot_general(a, b, (((0,), (0,)), ((), ())), preferred_element_type=jnp.float32)


def nn(a, b):
    return jnp.dot(a, b, preferred_element_type=jnp.float32)


def merge(parts, count):
    t_top = parts[0, 0:1]
    s_top = parts[0, 1:2]
    for i in range(1, count):
        t_top = jnp.maximum(t_top, parts[i, 0:1])
        s_top = jnp.maximum(s_top, parts[i, 1:2])
    t_sum = jnp.zeros_like(t_top)
    s_sum = jnp.zeros_like(t_top)
    cross = jnp.zeros_like(t_top)
    for i in range(count):
        t_scale = jnp.exp(parts[i, 0:1] - t_top)
        t_sum += parts[i, 2:3] * t_scale
        cross += parts[i, 4:5] * t_scale
        s_sum += parts[i, 3:4] * jnp.exp(parts[i, 1:2] - s_top)
    return t_top, s_top, t_sum, s_sum, cross


def main_kernel(
    n, nv, rows, live, cuts, npieces,
    sh_ref, th_ref, live_ref, count_ref, dest_ref, shead_hbm, thead_hbm,
    loss_ref, ghead_ref, gh_ref, *scratch,
):
    bufs, scratch = scratch[:npieces], scratch[npieces:]
    (
        gm, shead, thead, onehot_s, onehot_t, hc_ref, s_log, t_log,
        st, sz, lgx, core_out, core_in, mine, plane_out, plane_in, own, z_out, z_in,
        head_sem, m_send, m_recv, ici_send, core_send, g_recv, relay_send, relay_recv,
        st_send, st_recv, sz_send, sz_recv, c_send, c_recv, p_send, p_recv, z_send, z_recv,
    ) = scratch
    nc = n // 2
    me = lax.axis_index("dp")
    vi = lax.axis_index("vocab")
    core = lax.rem(me, 2)
    chip = lax.div(me, 2)
    partner = 2 * chip + 1 - core
    pair = 2 * rows
    width = n * pair
    ds, dt = shead.shape[0], thead.shape[0]

    head_copies = [
        pltpu.make_async_copy(shead_hbm, shead, head_sem.at[0]),
        pltpu.make_async_copy(thead_hbm, thead, head_sem.at[1]),
    ]
    for copy in head_copies:
        copy.start()

    barrier = pltpu.get_barrier_semaphore()
    for r in range(1, n):
        pl.semaphore_signal(barrier, inc=1, device_id={"dp": lax.rem(me + r, n)}, device_id_type=MESH)
    for r in range(1, nv):
        pl.semaphore_signal(barrier, inc=1, device_id={"vocab": lax.rem(vi + r, nv)}, device_id_type=MESH)

    lane = lax.broadcasted_iota(jnp.int32, (1, width), 1)
    half_l = jnp.zeros((1, width), jnp.int32)
    shard_l = jnp.zeros((1, width), jnp.int32)
    pos_l = lane
    for i in range(1, 2 * n):
        pos_l = jnp.where(lane >= i * rows, lane - i * rows, pos_l)
        half_l = jnp.where(lane >= i * rows, i % 2, half_l)
        shard_l = jnp.where(lane >= i * rows, i // 2, shard_l)
    dest_l = jnp.zeros((1, width), jnp.int32)
    for i in range(rows):
        dest_l = jnp.where(pos_l == i, dest_ref[i], dest_l)
    here = shard_l == me
    gm[me] = jnp.concatenate(
        [
            jnp.where(here, live_ref[0], 0),
            jnp.where(shard_l > me, live_ref[0], 0),
            jnp.where(here, count_ref[0], 0),
            jnp.where(here, dest_l, 0),
            jnp.zeros((4, width), jnp.int32),
        ],
        axis=0,
    )
    for i, (b, at, size) in enumerate(cuts):
        ref = (sh_ref, th_ref)[b]
        half = ref.shape[1] // 2
        left = ref[:, at:at + size].astype(jnp.float32)
        right = ref[:, half + at:half + at + size].astype(jnp.float32)
        bufs[i][me] = jnp.concatenate([left, right], axis=0).astype(jnp.bfloat16)
    pl.semaphore_wait(barrier, n - 1 + nv - 1)

    def remote(src, dst, send, recv, target):
        return pltpu.make_async_remote_copy(
            src_ref=src, dst_ref=dst, send_sem=send, recv_sem=recv,
            device_id=target, device_id_type=MESH,
        )

    waits = []

    def go(copy):
        copy.start()
        waits.append(copy)

    for r in range(1, n):
        target = lax.rem(me + r, n)
        go(remote(gm.at[me], gm.at[me], m_send.at[r], m_recv.at[me], {"dp": target}))
    square = nc == 4
    x_chip = 2 * lax.div(chip, 2) + 1 - lax.rem(chip, 2)
    y_chip = lax.rem(chip + 2, 4)
    targets = [x_chip, y_chip] if square else [lax.rem(chip + r, nc) for r in range(1, nc)]
    sources = [x_chip, y_chip] if square else [lax.rem(chip + nc - r, nc) for r in range(1, nc)]

    def block_copy(i, shard, send, target):
        return remote(bufs[i].at[shard], bufs[i].at[shard], send, g_recv.at[i, shard], {"dp": target})

    def start_own(i):
        for r, to in enumerate(targets):
            go(block_copy(i, me, ici_send.at[i, r], 2 * to + core))
        go(block_copy(i, me, core_send.at[i, 0], partner))

    def pass_on(i):
        for r, source in enumerate(sources):
            shard = 2 * source + core
            block_copy(i, shard, core_send.at[i, r + 1], partner).wait_recv()
            if square:
                size = bufs[i].shape[2] // 2
                to = (y_chip, x_chip)[r]
                part = bufs[i].at[shard, :, pl.ds(r * size, size)]
                go(remote(part, part, relay_send.at[i, r], relay_recv.at[i, r], {"dp": 2 * to + core}))
            go(block_copy(i, shard, core_send.at[i, r + 1], partner))

    def finish(i):
        if square:
            shard = 2 * (3 - chip) + core
            for r in range(2):
                size = bufs[i].shape[2] // 2
                part = bufs[i].at[shard, :, pl.ds(r * size, size)]
                remote(part, part, relay_send.at[i, r], relay_recv.at[i, r], {"dp": partner}).wait_recv()
            go(block_copy(i, shard, core_send.at[i, 3], partner))
        for c in range(nc):
            block_copy(i, 2 * c + 1 - core, core_send.at[i, 0], partner).wait_recv()

    start_own(0)
    start_own(1)
    for r in range(1, n):
        shard = lax.rem(me + r, n)
        remote(gm.at[shard], gm.at[shard], m_send.at[r], m_recv.at[shard], {"dp": shard}).wait_recv()
    meta = gm[0]
    for i in range(1, n):
        meta = meta + gm[i]
    live_l, off_l, count_l, dest_l = meta[0:1], meta[1:2], meta[2:3], meta[3:4]

    rank_l = jnp.zeros((1, width), jnp.int32)
    for i in range(n):
        off_i = off_l[:, i * pair:i * pair + 1]
        inside = (dest_l >= i * rows) & (dest_l < (i + 1) * rows)
        rank_l = jnp.where(inside, dest_l - i * rows + off_i, rank_l)
    shape = (2 * live, width)
    row = lax.broadcasted_iota(jnp.int32, shape, 0)
    key_s = jnp.where(pos_l < live_l, pos_l + off_l + live * half_l, -1)
    key_t = jnp.where(pos_l < count_l, rank_l + live * half_l, -1)
    onehot_s[...] = jnp.where(row == key_s, 1.0, 0.0).astype(jnp.bfloat16)
    onehot_t[...] = jnp.where(row == key_t, 1.0, 0.0).astype(jnp.bfloat16)

    def logits(i):
        b, at, size = cuts[i]
        onehot, head, out = ((onehot_s, shead, s_log), (onehot_t, thead, t_log))[b]
        half = head.shape[0] // 2
        packed = nn(onehot[...], bufs[i][...].reshape(width, size)).astype(jnp.bfloat16)
        top, low = packed[:live], packed[live:]
        if b == 0:
            hc_ref[:, at:at + size] = top
            hc_ref[:, half + at:half + at + size] = low
        value = nn(top, head[at:at + size, :]) + nn(low, head[half + at:half + at + size, :])
        out[...] = value if at == 0 else out[...] + value

    for i in range(npieces + 1):
        if i < npieces:
            pass_on(i)
            if i + 2 < npieces:
                start_own(i + 2)
        if i >= 1:
            finish(i - 1)
            b, at, _ = cuts[i - 1]
            if at == 0:
                head_copies[b].wait()
            logits(i - 1)

    lanes = st.shape[2]
    s_val, t_val = s_log[...], t_log[...]
    t_top = jnp.max(t_val, axis=1, keepdims=True)
    s_top = jnp.max(s_val, axis=1, keepdims=True)
    t_exp = jnp.exp(t_val - t_top)
    t_sum = jnp.sum(t_exp, axis=1, keepdims=True)
    s_sum = jnp.sum(jnp.exp(s_val - s_top), axis=1, keepdims=True)
    cross = jnp.sum(t_exp * (t_val - s_val), axis=1, keepdims=True)
    col = lax.broadcasted_iota(jnp.int32, (live, 128), 1)
    table = jnp.where(col == 0, t_top, 1.0)
    for i, value in ((1, s_top), (2, t_sum), (3, s_sum), (4, cross)):
        table = jnp.where(col == i, value, table)
    if lanes > live:
        table = jnp.concatenate([table, jnp.ones((lanes - live, 128), jnp.float32)], axis=0)
    st[me] = jnp.transpose(table)[0:8]
    for r in range(1, n):
        go(remote(st.at[me], st.at[me], st_send.at[r], st_recv.at[me], {"dp": lax.rem(me + r, n)}))
    for r in range(1, n):
        shard = lax.rem(me + r, n)
        remote(st.at[shard], st.at[shard], st_send.at[r], st_recv.at[shard], {"dp": shard}).wait_recv()
    joined = merge(st, n)
    ones = jnp.ones((3, lanes), jnp.float32)
    sz[vi] = jnp.concatenate(list(joined) + [ones], axis=0)
    for r in range(1, nv):
        go(remote(sz.at[vi], sz.at[vi], sz_send.at[r], sz_recv.at[vi], {"vocab": lax.rem(vi + r, nv)}))
    for r in range(1, nv):
        shard = lax.rem(vi + r, nv)
        remote(sz.at[shard], sz.at[shard], sz_send.at[r], sz_recv.at[shard], {"vocab": shard}).wait_recv()
    t_top, s_top, t_sum, s_sum, cross = merge(sz, nv)
    t_norm = t_top + jnp.log(t_sum)
    s_norm = s_top + jnp.log(s_sum)
    divergence = cross / t_sum - t_norm + s_norm
    lane = lax.broadcasted_iota(jnp.int32, (1, lanes), 1)
    divergence = jnp.where(lane < live, divergence, 0.0)
    loss_ref[...] = jnp.sum(divergence, axis=1, keepdims=True) / live
    norms = jnp.concatenate([t_norm, s_norm, jnp.zeros((126, lanes), jnp.float32)], axis=0)
    norms = jnp.transpose(norms)[:live]
    gap = jnp.exp(s_val - norms[:, 1:2]) - jnp.exp(t_val - norms[:, 0:1])
    grad = (gap * (loss_scale / live)).astype(jnp.bfloat16)

    spread = tn(onehot_s[0:live, :], grad)
    sides = [
        jnp.concatenate([spread[(2 * c + k) * pair:(2 * c + k) * pair + rows] for c in range(nc)], axis=0)
        for k in range(2)
    ]
    is_zero = core == 0
    lgx[0:nc * rows] = jnp.where(is_zero, sides[1], sides[0]).astype(jnp.bfloat16)
    lgx[nc * rows:] = jnp.where(is_zero, sides[0], sides[1]).astype(jnp.bfloat16)

    half = core_out.shape[3]

    for j in range(nv):
        base = pl.multiple_of(lax.rem(vi + 1 + j, nv) * (2 * half), 16)
        low = nt(lgx[...], shead[pl.ds(base, half), :])
        high = nt(lgx[...], shead[pl.ds(pl.multiple_of(base + half, 16), half), :])
        blocks = [
            jnp.concatenate([low[c * rows:(c + 1) * rows], high[c * rows:(c + 1) * rows]], axis=0)
            for c in range(2 * nc)
        ]
        for c in range(nc):
            core_out[j, c] = blocks[c].astype(jnp.bfloat16)
        go(remote(core_out.at[j], core_in.at[j], c_send.at[j], c_recv.at[j], {"dp": partner}))
        for c in range(nc):
            mine[j, c] = blocks[nc + c]
    for j in range(nv):
        remote(core_out.at[j], core_in.at[j], c_send.at[j], c_recv.at[j], {"dp": partner}).wait_recv()
        mine[j] = mine[j] + core_in[j].astype(jnp.float32)
        plane_out[j] = mine[j].astype(jnp.bfloat16)
        for r in range(1, nc):
            to = lax.rem(chip + r, nc)
            go(remote(plane_out.at[j, to], plane_in.at[j, r], p_send.at[j, r], p_recv.at[j, r], {"dp": 2 * to + core}))
    tile = 512
    slabs = ds // tile
    for j in range(nv):
        for i in range(slabs * j // nv, slabs * (j + 1) // nv):
            ghead_ref[i * tile:(i + 1) * tile, :] = tn(hc_ref[:, i * tile:(i + 1) * tile], grad).astype(jnp.bfloat16)
        total = mine[j, chip]
        for r in range(1, nc):
            remote(plane_in.at[j, r], plane_in.at[j, r], p_send.at[j, r], p_recv.at[j, r], {"dp": partner}).wait_recv()
            total = total + plane_in[j, r].astype(jnp.float32)
        if j < nv - 1:
            z_out[j] = total.astype(jnp.bfloat16)
            go(remote(z_out.at[j], z_in.at[j], z_send.at[j], z_recv.at[j], {"vocab": lax.rem(vi + 1 + j, nv)}))
        else:
            own[...] = total
    total = own[...]
    for j in range(nv - 1):
        remote(z_in.at[j], z_in.at[j], z_send.at[j], z_recv.at[j], {"vocab": lax.rem(vi + 1, nv)}).wait_recv()
        total = total + z_in[j].astype(jnp.float32)
    gh_ref[...] = total.astype(jnp.bfloat16)
    for copy in waits:
        copy.wait_send()


def per_device(
    student_hidden,
    teacher_hidden,
    student_head,
    teacher_head,
    live_count,
    teacher_count,
    teacher_dest,
):
    rows, ds = student_hidden.shape
    dt = teacher_hidden.shape[1]
    vocab = student_head.shape[1]
    n = lax.axis_size("dp")
    nv = lax.axis_size("vocab")
    nc = n // 2
    live = rows * n // 2
    lanes = -(-live // 128) * 128
    pair = 2 * rows
    width = n * pair
    half = ds // nv // 2
    bf16, f32 = jnp.bfloat16, jnp.float32
    vmem = pl.BlockSpec(memory_space=pltpu.VMEM)
    hbm = pl.BlockSpec(memory_space=pltpu.HBM)
    dma = pltpu.SemaphoreType.DMA
    smem = pl.BlockSpec(memory_space=pltpu.SMEM)
    cuts = []
    for b, sizes in enumerate(((1024, 768), (768, 768, 768))):
        at = 0
        for size in sizes:
            cuts.append((b, at, size))
            at += size
        assert at == (ds, dt)[b] // 2
    pieces = len(cuts)
    loss, grad_head, gh = pl.pallas_call(
        functools.partial(main_kernel, n, nv, rows, live, cuts, pieces),
        out_shape=(
            jax.ShapeDtypeStruct((1, 1), f32),
            pltpu.VMEM((ds, vocab), bf16),
            jax.ShapeDtypeStruct((pair, half), bf16),
        ),
        in_specs=[vmem, vmem, smem, smem, smem, hbm, hbm],
        out_specs=(vmem, vmem, vmem),
        scratch_shapes=[
            *[pltpu.VMEM((n, pair, size), bf16) for _, _, size in cuts],
            pltpu.VMEM((n, 8, width), jnp.int32),
            pltpu.VMEM((ds, vocab), bf16),
            pltpu.VMEM((dt, vocab), bf16),
            pltpu.VMEM((2 * live, width), bf16),
            pltpu.VMEM((2 * live, width), bf16),
            pltpu.VMEM((live, ds), bf16),
            pltpu.VMEM((live, vocab), f32),
            pltpu.VMEM((live, vocab), f32),
            pltpu.VMEM((n, 8, lanes), f32),
            pltpu.VMEM((nv, 8, lanes), f32),
            pltpu.VMEM((2 * nc * rows, vocab), bf16),
            pltpu.VMEM((nv, nc, pair, half), bf16),
            pltpu.VMEM((nv, nc, pair, half), bf16),
            pltpu.VMEM((nv, nc, pair, half), f32),
            pltpu.VMEM((nv, nc, pair, half), bf16),
            pltpu.VMEM((nv, nc, pair, half), bf16),
            pltpu.VMEM((pair, half), f32),
            pltpu.VMEM((nv, pair, half), bf16),
            pltpu.VMEM((nv, pair, half), bf16),
            dma((2,)),
            dma((n,)), dma((n,)),
            dma((pieces, nc)), dma((pieces, nc)), dma((pieces, n)), dma((pieces, 2)), dma((pieces, 2)),
            dma((n,)), dma((n,)), dma((nv,)), dma((nv,)),
            dma((nv,)), dma((nv,)), dma((nv, nc)), dma((nv, nc)), dma((nv,)), dma((nv,)),
        ],
        compiler_params=pltpu.CompilerParams(
            collective_id=0, has_side_effects=True, vmem_limit_bytes=(56 if n <= 8 else 58) * 2**20
        ),
        name="distill",
    )(student_hidden, teacher_hidden, live_count, teacher_count, teacher_dest, student_head, teacher_head)
    grad_hidden = jnp.concatenate([gh[:rows], gh[rows:]], axis=1)
    return (loss[0, 0], grad_hidden, grad_head)


def solution(mesh):
    return jax.shard_map(
        per_device,
        mesh=mesh,
        in_specs=(
            P("dp", None),
            P("dp", None),
            P(None, ("dp", "vocab")),
            P(None, ("dp", "vocab")),
            P("dp"),
            P("dp"),
            P("dp"),
        ),
        out_specs=(P(), P("dp", "vocab"), P(None, ("dp", "vocab"))),
        check_vma=False,
    )
```

```python
import functools

import jax
import jax.numpy as jnp
from jax import lax
from jax.experimental import pallas as pl
from jax.experimental.pallas import tpu as pltpu
from jax.sharding import PartitionSpec as P

loss_scale = 65536.0
MESH = pl.DeviceIdType.MESH


def nt(a, b):
    return lax.dot_general(a, b, (((1,), (1,)), ((), ())), preferred_element_type=jnp.float32)


def tn(a, b):
    return lax.dot_general(a, b, (((0,), (0,)), ((), ())), preferred_element_type=jnp.float32)


def nn(a, b):
    return jnp.dot(a, b, preferred_element_type=jnp.float32)


def merge(parts, count):
    t_top = parts[0, 0:1]
    s_top = parts[0, 1:2]
    for i in range(1, count):
        t_top = jnp.maximum(t_top, parts[i, 0:1])
        s_top = jnp.maximum(s_top, parts[i, 1:2])
    t_sum = jnp.zeros_like(t_top)
    s_sum = jnp.zeros_like(t_top)
    cross = jnp.zeros_like(t_top)
    for i in range(count):
        t_scale = jnp.exp(parts[i, 0:1] - t_top)
        t_sum += parts[i, 2:3] * t_scale
        cross += parts[i, 4:5] * t_scale
        s_sum += parts[i, 3:4] * jnp.exp(parts[i, 1:2] - s_top)
    return t_top, s_top, t_sum, s_sum, cross


def main_kernel(
    n, nv, rows, live, cuts, npieces,
    sh_ref, th_ref, live_ref, count_ref, dest_ref, shead_hbm, thead_hbm,
    loss_ref, ghead_ref, gh_ref, *scratch,
):
    bufs, scratch = scratch[:npieces], scratch[npieces:]
    (
        gm, shead, thead, onehot_s, onehot_t, hc_ref, s_log, t_log,
        st, sz, lgx, core_out, core_in, mine, plane_out, plane_in, own, z_out, z_in,
        head_sem, m_send, m_recv, ici_send, core_send, g_recv, relay_send, relay_recv,
        st_send, st_recv, sz_send, sz_recv, c_send, c_recv, p_send, p_recv, z_send, z_recv,
    ) = scratch
    nc = n // 2
    me = lax.axis_index("dp")
    vi = lax.axis_index("vocab")
    core = lax.rem(me, 2)
    chip = lax.div(me, 2)
    partner = 2 * chip + 1 - core
    pair = 2 * rows
    width = n * pair
    ds, dt = shead.shape[0], thead.shape[0]

    head_copies = [
        pltpu.make_async_copy(shead_hbm, shead, head_sem.at[0]),
        pltpu.make_async_copy(thead_hbm, thead, head_sem.at[1]),
    ]
    for copy in head_copies:
        copy.start()

    barrier = pltpu.get_barrier_semaphore()
    for r in range(1, n):
        pl.semaphore_signal(barrier, inc=1, device_id={"dp": lax.rem(me + r, n)}, device_id_type=MESH)
    for r in range(1, nv):
        pl.semaphore_signal(barrier, inc=1, device_id={"vocab": lax.rem(vi + r, nv)}, device_id_type=MESH)

    def fold(i):
        b, at, size = cuts[i]
        ref = (sh_ref, th_ref)[b]
        half = ref.shape[1] // 2
        left = ref[:, at:at + size].astype(jnp.float32)
        right = ref[:, half + at:half + at + size].astype(jnp.float32)
        bufs[i][me] = jnp.concatenate([left, right], axis=0).astype(jnp.bfloat16)

    fold(0)
    pl.semaphore_wait(barrier, n - 1 + nv - 1)

    def remote(src, dst, send, recv, target):
        return pltpu.make_async_remote_copy(
            src_ref=src, dst_ref=dst, send_sem=send, recv_sem=recv,
            device_id=target, device_id_type=MESH,
        )

    waits = []

    def go(copy):
        copy.start()
        waits.append(copy)

    square = nc == 4
    x_chip = 2 * lax.div(chip, 2) + 1 - lax.rem(chip, 2)
    y_chip = lax.rem(chip + 2, 4)
    targets = [x_chip, y_chip] if square else [lax.rem(chip + r, nc) for r in range(1, nc)]
    sources = [x_chip, y_chip] if square else [lax.rem(chip + nc - r, nc) for r in range(1, nc)]

    def block_copy(i, shard, send, target):
        return remote(bufs[i].at[shard], bufs[i].at[shard], send, g_recv.at[i, shard], {"dp": target})

    def start_own(i):
        for r, to in enumerate(targets):
            go(block_copy(i, me, ici_send.at[i, r], 2 * to + core))
        go(block_copy(i, me, core_send.at[i, 0], partner))

    def pass_on(i):
        for r, source in enumerate(sources):
            shard = 2 * source + core
            block_copy(i, shard, core_send.at[i, r + 1], partner).wait_recv()
            if square:
                size = bufs[i].shape[2] // 2
                to = (y_chip, x_chip)[r]
                part = bufs[i].at[shard, :, pl.ds(r * size, size)]
                go(remote(part, part, relay_send.at[i, r], relay_recv.at[i, r], {"dp": 2 * to + core}))
            go(block_copy(i, shard, core_send.at[i, r + 1], partner))

    def finish(i):
        if square:
            shard = 2 * (3 - chip) + core
            for r in range(2):
                size = bufs[i].shape[2] // 2
                part = bufs[i].at[shard, :, pl.ds(r * size, size)]
                remote(part, part, relay_send.at[i, r], relay_recv.at[i, r], {"dp": partner}).wait_recv()
            go(block_copy(i, shard, core_send.at[i, 3], partner))
        for c in range(nc):
            block_copy(i, 2 * c + 1 - core, core_send.at[i, 0], partner).wait_recv()

    start_own(0)
    fold(1)
    start_own(1)
    lane = lax.broadcasted_iota(jnp.int32, (1, width), 1)
    half_l = jnp.zeros((1, width), jnp.int32)
    shard_l = jnp.zeros((1, width), jnp.int32)
    pos_l = lane
    for i in range(1, 2 * n):
        pos_l = jnp.where(lane >= i * rows, lane - i * rows, pos_l)
        half_l = jnp.where(lane >= i * rows, i % 2, half_l)
        shard_l = jnp.where(lane >= i * rows, i // 2, shard_l)
    dest_l = jnp.zeros((1, width), jnp.int32)
    for i in range(rows):
        dest_l = jnp.where(pos_l == i, dest_ref[i], dest_l)
    here = shard_l == me
    gm[me] = jnp.concatenate(
        [
            jnp.where(here, live_ref[0], 0),
            jnp.where(shard_l > me, live_ref[0], 0),
            jnp.where(here, count_ref[0], 0),
            jnp.where(here, dest_l, 0),
            jnp.zeros((4, width), jnp.int32),
        ],
        axis=0,
    )
    for r in range(1, n):
        target = lax.rem(me + r, n)
        go(remote(gm.at[me], gm.at[me], m_send.at[r], m_recv.at[me], {"dp": target}))
    for i in range(2, npieces):
        fold(i)
    for r in range(1, n):
        shard = lax.rem(me + r, n)
        remote(gm.at[shard], gm.at[shard], m_send.at[r], m_recv.at[shard], {"dp": shard}).wait_recv()
    meta = gm[0]
    for i in range(1, n):
        meta = meta + gm[i]
    live_l, off_l, count_l, dest_l = meta[0:1], meta[1:2], meta[2:3], meta[3:4]

    rank_l = jnp.zeros((1, width), jnp.int32)
    for i in range(n):
        off_i = off_l[:, i * pair:i * pair + 1]
        inside = (dest_l >= i * rows) & (dest_l < (i + 1) * rows)
        rank_l = jnp.where(inside, dest_l - i * rows + off_i, rank_l)
    shape = (2 * live, width)
    row = lax.broadcasted_iota(jnp.int32, shape, 0)
    key_s = jnp.where(pos_l < live_l, pos_l + off_l + live * half_l, -1)
    key_t = jnp.where(pos_l < count_l, rank_l + live * half_l, -1)
    onehot_s[...] = jnp.where(row == key_s, 1.0, 0.0).astype(jnp.bfloat16)
    onehot_t[...] = jnp.where(row == key_t, 1.0, 0.0).astype(jnp.bfloat16)

    def logits(i):
        b, at, size = cuts[i]
        onehot, head, out = ((onehot_s, shead, s_log), (onehot_t, thead, t_log))[b]
        half = head.shape[0] // 2
        packed = nn(onehot[...], bufs[i][...].reshape(width, size)).astype(jnp.bfloat16)
        top, low = packed[:live], packed[live:]
        if b == 0:
            hc_ref[:, at:at + size] = top
            hc_ref[:, half + at:half + at + size] = low
        value = nn(top, head[at:at + size, :]) + nn(low, head[half + at:half + at + size, :])
        out[...] = value if at == 0 else out[...] + value

    for i in range(npieces + 1):
        if i < npieces:
            pass_on(i)
            if i + 2 < npieces:
                start_own(i + 2)
        if i >= 1:
            finish(i - 1)
            b, at, _ = cuts[i - 1]
            if at == 0:
                head_copies[b].wait()
            logits(i - 1)

    lanes = st.shape[2]
    s_val, t_val = s_log[...], t_log[...]
    t_top = jnp.max(t_val, axis=1, keepdims=True)
    s_top = jnp.max(s_val, axis=1, keepdims=True)
    t_exp = jnp.exp(t_val - t_top)
    t_sum = jnp.sum(t_exp, axis=1, keepdims=True)
    s_sum = jnp.sum(jnp.exp(s_val - s_top), axis=1, keepdims=True)
    cross = jnp.sum(t_exp * (t_val - s_val), axis=1, keepdims=True)
    col = lax.broadcasted_iota(jnp.int32, (live, 128), 1)
    table = jnp.where(col == 0, t_top, 1.0)
    for i, value in ((1, s_top), (2, t_sum), (3, s_sum), (4, cross)):
        table = jnp.where(col == i, value, table)
    if lanes > live:
        table = jnp.concatenate([table, jnp.ones((lanes - live, 128), jnp.float32)], axis=0)
    st[me] = jnp.transpose(table)[0:8]
    for r in range(1, n):
        go(remote(st.at[me], st.at[me], st_send.at[r], st_recv.at[me], {"dp": lax.rem(me + r, n)}))
    for r in range(1, n):
        shard = lax.rem(me + r, n)
        remote(st.at[shard], st.at[shard], st_send.at[r], st_recv.at[shard], {"dp": shard}).wait_recv()
    joined = merge(st, n)
    ones = jnp.ones((3, lanes), jnp.float32)
    sz[vi] = jnp.concatenate(list(joined) + [ones], axis=0)
    for r in range(1, nv):
        go(remote(sz.at[vi], sz.at[vi], sz_send.at[r], sz_recv.at[vi], {"vocab": lax.rem(vi + r, nv)}))
    for r in range(1, nv):
        shard = lax.rem(vi + r, nv)
        remote(sz.at[shard], sz.at[shard], sz_send.at[r], sz_recv.at[shard], {"vocab": shard}).wait_recv()
    t_top, s_top, t_sum, s_sum, cross = merge(sz, nv)
    t_norm = t_top + jnp.log(t_sum)
    s_norm = s_top + jnp.log(s_sum)
    divergence = cross / t_sum - t_norm + s_norm
    lane = lax.broadcasted_iota(jnp.int32, (1, lanes), 1)
    divergence = jnp.where(lane < live, divergence, 0.0)
    loss_ref[...] = jnp.sum(divergence, axis=1, keepdims=True) / live
    norms = jnp.concatenate([t_norm, s_norm, jnp.zeros((126, lanes), jnp.float32)], axis=0)
    norms = jnp.transpose(norms)[:live]
    gap = jnp.exp(s_val - norms[:, 1:2]) - jnp.exp(t_val - norms[:, 0:1])
    grad = (gap * (loss_scale / live)).astype(jnp.bfloat16)

    spread = tn(onehot_s[0:live, :], grad)
    sides = [
        jnp.concatenate([spread[(2 * c + k) * pair:(2 * c + k) * pair + rows] for c in range(nc)], axis=0)
        for k in range(2)
    ]
    is_zero = core == 0
    lgx[0:nc * rows] = jnp.where(is_zero, sides[1], sides[0]).astype(jnp.bfloat16)
    lgx[nc * rows:] = jnp.where(is_zero, sides[0], sides[1]).astype(jnp.bfloat16)

    half = core_out.shape[3]

    def partial(j):
        base = pl.multiple_of(lax.rem(vi + 1 + j, nv) * (2 * half), 16)
        low = nt(lgx[...], shead[pl.ds(base, half), :])
        high = nt(lgx[...], shead[pl.ds(pl.multiple_of(base + half, 16), half), :])
        blocks = [
            jnp.concatenate([low[c * rows:(c + 1) * rows], high[c * rows:(c + 1) * rows]], axis=0)
            for c in range(2 * nc)
        ]
        for c in range(nc):
            core_out[j, c] = blocks[c].astype(jnp.bfloat16)
        go(remote(core_out.at[j], core_in.at[j], c_send.at[j], c_recv.at[j], {"dp": partner}))
        for c in range(nc):
            mine[j, c] = blocks[nc + c]

    def to_plane(j):
        remote(core_out.at[j], core_in.at[j], c_send.at[j], c_recv.at[j], {"dp": partner}).wait_recv()
        mine[j] = mine[j] + core_in[j].astype(jnp.float32)
        plane_out[j] = mine[j].astype(jnp.bfloat16)
        for r in range(1, nc):
            to = lax.rem(chip + r, nc)
            go(remote(plane_out.at[j, to], plane_in.at[j, r], p_send.at[j, r], p_recv.at[j, r], {"dp": 2 * to + core}))

    for j in range(nv + 1):
        if j < nv:
            partial(j)
        if j >= 1:
            to_plane(j - 1)
    tile = 512
    slabs = ds // tile
    for j in range(nv):
        for i in range(slabs * j // nv, slabs * (j + 1) // nv):
            ghead_ref[i * tile:(i + 1) * tile, :] = tn(hc_ref[:, i * tile:(i + 1) * tile], grad).astype(jnp.bfloat16)
        total = mine[j, chip]
        for r in range(1, nc):
            remote(plane_in.at[j, r], plane_in.at[j, r], p_send.at[j, r], p_recv.at[j, r], {"dp": partner}).wait_recv()
            total = total + plane_in[j, r].astype(jnp.float32)
        if j < nv - 1:
            z_out[j] = total.astype(jnp.bfloat16)
            go(remote(z_out.at[j], z_in.at[j], z_send.at[j], z_recv.at[j], {"vocab": lax.rem(vi + 1 + j, nv)}))
        else:
            own[...] = total
    total = own[...]
    for j in range(nv - 1):
        remote(z_in.at[j], z_in.at[j], z_send.at[j], z_recv.at[j], {"vocab": lax.rem(vi + 1, nv)}).wait_recv()
        total = total + z_in[j].astype(jnp.float32)
    gh_ref[...] = jnp.concatenate([total[:rows], total[rows:]], axis=1).astype(jnp.bfloat16)
    for copy in waits:
        copy.wait_send()


def per_device(
    student_hidden,
    teacher_hidden,
    student_head,
    teacher_head,
    live_count,
    teacher_count,
    teacher_dest,
):
    rows, ds = student_hidden.shape
    dt = teacher_hidden.shape[1]
    vocab = student_head.shape[1]
    n = lax.axis_size("dp")
    nv = lax.axis_size("vocab")
    nc = n // 2
    live = rows * n // 2
    lanes = -(-live // 128) * 128
    pair = 2 * rows
    width = n * pair
    half = ds // nv // 2
    bf16, f32 = jnp.bfloat16, jnp.float32
    vmem = pl.BlockSpec(memory_space=pltpu.VMEM)
    hbm = pl.BlockSpec(memory_space=pltpu.HBM)
    dma = pltpu.SemaphoreType.DMA
    smem = pl.BlockSpec(memory_space=pltpu.SMEM)
    cuts = []
    for b, sizes in enumerate(((1024, 768), (768, 768, 768))):
        at = 0
        for size in sizes:
            cuts.append((b, at, size))
            at += size
        assert at == (ds, dt)[b] // 2
    pieces = len(cuts)
    loss, grad_head, grad_hidden = pl.pallas_call(
        functools.partial(main_kernel, n, nv, rows, live, cuts, pieces),
        out_shape=(
            jax.ShapeDtypeStruct((1, 1), f32),
            pltpu.VMEM((ds, vocab), bf16),
            pltpu.VMEM((rows, 2 * half), bf16),
        ),
        in_specs=[vmem, vmem, smem, smem, smem, hbm, hbm],
        out_specs=(vmem, vmem, vmem),
        scratch_shapes=[
            *[pltpu.VMEM((n, pair, size), bf16) for _, _, size in cuts],
            pltpu.VMEM((n, 8, width), jnp.int32),
            pltpu.VMEM((ds, vocab), bf16),
            pltpu.VMEM((dt, vocab), bf16),
            pltpu.VMEM((2 * live, width), bf16),
            pltpu.VMEM((2 * live, width), bf16),
            pltpu.VMEM((live, ds), bf16),
            pltpu.VMEM((live, vocab), f32),
            pltpu.VMEM((live, vocab), f32),
            pltpu.VMEM((n, 8, lanes), f32),
            pltpu.VMEM((nv, 8, lanes), f32),
            pltpu.VMEM((2 * nc * rows, vocab), bf16),
            pltpu.VMEM((nv, nc, pair, half), bf16),
            pltpu.VMEM((nv, nc, pair, half), bf16),
            pltpu.VMEM((nv, nc, pair, half), f32),
            pltpu.VMEM((nv, nc, pair, half), bf16),
            pltpu.VMEM((nv, nc, pair, half), bf16),
            pltpu.VMEM((pair, half), f32),
            pltpu.VMEM((nv, pair, half), bf16),
            pltpu.VMEM((nv, pair, half), bf16),
            dma((2,)),
            dma((n,)), dma((n,)),
            dma((pieces, nc)), dma((pieces, nc)), dma((pieces, n)), dma((pieces, 2)), dma((pieces, 2)),
            dma((n,)), dma((n,)), dma((nv,)), dma((nv,)),
            dma((nv,)), dma((nv,)), dma((nv, nc)), dma((nv, nc)), dma((nv,)), dma((nv,)),
        ],
        compiler_params=pltpu.CompilerParams(
            collective_id=0, has_side_effects=True, vmem_limit_bytes=(56 if n <= 8 else 58) * 2**20
        ),
        name="distill",
    )(student_hidden, teacher_hidden, live_count, teacher_count, teacher_dest, student_head, teacher_head)
    return (loss[0, 0], grad_hidden, grad_head)


def solution(mesh):
    return jax.shard_map(
        per_device,
        mesh=mesh,
        in_specs=(
            P("dp", None),
            P("dp", None),
            P(None, ("dp", "vocab")),
            P(None, ("dp", "vocab")),
            P("dp"),
            P("dp"),
            P("dp"),
        ),
        out_specs=(P(), P("dp", "vocab"), P(None, ("dp", "vocab"))),
        check_vma=False,
    )
```

```python
import functools

import jax
import jax.numpy as jnp
from jax import lax
from jax.experimental import pallas as pl
from jax.experimental.pallas import tpu as pltpu
from jax.sharding import PartitionSpec as P

loss_scale = 65536.0
MESH = pl.DeviceIdType.MESH


def nt(a, b):
    return lax.dot_general(a, b, (((1,), (1,)), ((), ())), preferred_element_type=jnp.float32)


def tn(a, b):
    return lax.dot_general(a, b, (((0,), (0,)), ((), ())), preferred_element_type=jnp.float32)


def nn(a, b):
    return jnp.dot(a, b, preferred_element_type=jnp.float32)


def merge(parts, count):
    t_top = parts[0, 0:1]
    s_top = parts[0, 1:2]
    for i in range(1, count):
        t_top = jnp.maximum(t_top, parts[i, 0:1])
        s_top = jnp.maximum(s_top, parts[i, 1:2])
    t_sum = jnp.zeros_like(t_top)
    s_sum = jnp.zeros_like(t_top)
    cross = jnp.zeros_like(t_top)
    for i in range(count):
        t_scale = jnp.exp(parts[i, 0:1] - t_top)
        t_sum += parts[i, 2:3] * t_scale
        cross += parts[i, 4:5] * t_scale
        s_sum += parts[i, 3:4] * jnp.exp(parts[i, 1:2] - s_top)
    return t_top, s_top, t_sum, s_sum, cross


def main_kernel(
    n, nv, rows, live, cuts, npieces,
    sh_ref, th_ref, live_ref, count_ref, dest_ref, shead_hbm, thead_hbm,
    loss_ref, ghead_ref, gh_ref, *scratch,
):
    bufs, scratch = scratch[:npieces], scratch[npieces:]
    (
        gm, shead, thead, onehot_s, onehot_t, hc_ref, s_log, t_log,
        st, sz, lgx, core_out, core_in, mine, plane_out, plane_in, own, z_out, z_in,
        head_sem, m_send, m_recv, ici_send, core_send, g_recv, relay_send, relay_recv,
        st_send, st_recv, sz_send, sz_recv, c_send, c_recv, p_send, p_recv, z_send, z_recv,
    ) = scratch
    nc = n // 2
    me = lax.axis_index("dp")
    vi = lax.axis_index("vocab")
    core = lax.rem(me, 2)
    chip = lax.div(me, 2)
    partner = 2 * chip + 1 - core
    pair = 2 * rows
    width = n * pair
    ds, dt = shead.shape[0], thead.shape[0]

    head_copies = [
        pltpu.make_async_copy(shead_hbm, shead, head_sem.at[0]),
        pltpu.make_async_copy(thead_hbm, thead, head_sem.at[1]),
    ]
    for copy in head_copies:
        copy.start()

    barrier = pltpu.get_barrier_semaphore()
    for r in range(1, n):
        pl.semaphore_signal(barrier, inc=1, device_id={"dp": lax.rem(me + r, n)}, device_id_type=MESH)
    for r in range(1, nv):
        pl.semaphore_signal(barrier, inc=1, device_id={"vocab": lax.rem(vi + r, nv)}, device_id_type=MESH)

    def fold(i):
        b, at, size = cuts[i]
        ref = (sh_ref, th_ref)[b]
        half = ref.shape[1] // 2
        left = ref[:, at:at + size].astype(jnp.float32)
        right = ref[:, half + at:half + at + size].astype(jnp.float32)
        bufs[i][me] = jnp.concatenate([left, right], axis=0).astype(jnp.bfloat16)

    lane = lax.broadcasted_iota(jnp.int32, (1, width), 1)
    half_l = jnp.zeros((1, width), jnp.int32)
    shard_l = jnp.zeros((1, width), jnp.int32)
    pos_l = lane
    for i in range(1, 2 * n):
        pos_l = jnp.where(lane >= i * rows, lane - i * rows, pos_l)
        half_l = jnp.where(lane >= i * rows, i % 2, half_l)
        shard_l = jnp.where(lane >= i * rows, i // 2, shard_l)
    dest_l = jnp.zeros((1, width), jnp.int32)
    for i in range(rows):
        dest_l = jnp.where(pos_l == i, dest_ref[i], dest_l)
    here = shard_l == me
    gm[me] = jnp.concatenate(
        [
            jnp.where(here, live_ref[0], 0),
            jnp.where(shard_l > me, live_ref[0], 0),
            jnp.where(here, count_ref[0], 0),
            jnp.where(here, dest_l, 0),
            jnp.zeros((4, width), jnp.int32),
        ],
        axis=0,
    )
    fold(0)
    fold(1)
    pl.semaphore_wait(barrier, n - 1 + nv - 1)

    def remote(src, dst, send, recv, target):
        return pltpu.make_async_remote_copy(
            src_ref=src, dst_ref=dst, send_sem=send, recv_sem=recv,
            device_id=target, device_id_type=MESH,
        )

    waits = []

    def go(copy):
        copy.start()
        waits.append(copy)

    square = nc == 4
    x_chip = 2 * lax.div(chip, 2) + 1 - lax.rem(chip, 2)
    y_chip = lax.rem(chip + 2, 4)
    targets = [x_chip, y_chip] if square else [lax.rem(chip + r, nc) for r in range(1, nc)]
    sources = [x_chip, y_chip] if square else [lax.rem(chip + nc - r, nc) for r in range(1, nc)]

    def block_copy(i, shard, send, target):
        return remote(bufs[i].at[shard], bufs[i].at[shard], send, g_recv.at[i, shard], {"dp": target})

    def start_own(i):
        for r, to in enumerate(targets):
            go(block_copy(i, me, ici_send.at[i, r], 2 * to + core))
        go(block_copy(i, me, core_send.at[i, 0], partner))

    def pass_on(i):
        for r, source in enumerate(sources):
            shard = 2 * source + core
            block_copy(i, shard, core_send.at[i, r + 1], partner).wait_recv()
            if square:
                size = bufs[i].shape[2] // 2
                to = (y_chip, x_chip)[r]
                part = bufs[i].at[shard, :, pl.ds(r * size, size)]
                go(remote(part, part, relay_send.at[i, r], relay_recv.at[i, r], {"dp": 2 * to + core}))
            go(block_copy(i, shard, core_send.at[i, r + 1], partner))

    def finish(i):
        if square:
            shard = 2 * (3 - chip) + core
            for r in range(2):
                size = bufs[i].shape[2] // 2
                part = bufs[i].at[shard, :, pl.ds(r * size, size)]
                remote(part, part, relay_send.at[i, r], relay_recv.at[i, r], {"dp": partner}).wait_recv()
            go(block_copy(i, shard, core_send.at[i, 3], partner))
        for c in range(nc):
            block_copy(i, 2 * c + 1 - core, core_send.at[i, 0], partner).wait_recv()

    for r in range(1, n):
        target = lax.rem(me + r, n)
        go(remote(gm.at[me], gm.at[me], m_send.at[r], m_recv.at[me], {"dp": target}))
    start_own(0)
    start_own(1)
    for i in range(2, npieces):
        fold(i)
    pass_on(0)
    start_own(2)
    for r in range(1, n):
        shard = lax.rem(me + r, n)
        remote(gm.at[shard], gm.at[shard], m_send.at[r], m_recv.at[shard], {"dp": shard}).wait_recv()
    meta = gm[0]
    for i in range(1, n):
        meta = meta + gm[i]
    live_l, off_l, count_l, dest_l = meta[0:1], meta[1:2], meta[2:3], meta[3:4]

    rank_l = jnp.zeros((1, width), jnp.int32)
    for i in range(n):
        off_i = off_l[:, i * pair:i * pair + 1]
        inside = (dest_l >= i * rows) & (dest_l < (i + 1) * rows)
        rank_l = jnp.where(inside, dest_l - i * rows + off_i, rank_l)
    shape = (2 * live, width)
    row = lax.broadcasted_iota(jnp.int32, shape, 0)
    key_s = jnp.where(pos_l < live_l, pos_l + off_l + live * half_l, -1)
    key_t = jnp.where(pos_l < count_l, rank_l + live * half_l, -1)
    onehot_s[...] = jnp.where(row == key_s, 1.0, 0.0).astype(jnp.bfloat16)
    onehot_t[...] = jnp.where(row == key_t, 1.0, 0.0).astype(jnp.bfloat16)

    def logits(i):
        b, at, size = cuts[i]
        onehot, head, out = ((onehot_s, shead, s_log), (onehot_t, thead, t_log))[b]
        half = head.shape[0] // 2
        packed = nn(onehot[...], bufs[i][...].reshape(width, size)).astype(jnp.bfloat16)
        top, low = packed[:live], packed[live:]
        if b == 0:
            hc_ref[:, at:at + size] = top
            hc_ref[:, half + at:half + at + size] = low
        value = nn(top, head[at:at + size, :]) + nn(low, head[half + at:half + at + size, :])
        out[...] = value if at == 0 else out[...] + value

    for i in range(npieces + 1):
        if 0 < i < npieces:
            pass_on(i)
            if i + 2 < npieces:
                start_own(i + 2)
        if i >= 1:
            finish(i - 1)
            b, at, _ = cuts[i - 1]
            if at == 0:
                head_copies[b].wait()
            logits(i - 1)

    lanes = st.shape[2]
    s_val, t_val = s_log[...], t_log[...]
    t_top = jnp.max(t_val, axis=1, keepdims=True)
    s_top = jnp.max(s_val, axis=1, keepdims=True)
    t_exp = jnp.exp(t_val - t_top)
    t_sum = jnp.sum(t_exp, axis=1, keepdims=True)
    s_sum = jnp.sum(jnp.exp(s_val - s_top), axis=1, keepdims=True)
    cross = jnp.sum(t_exp * (t_val - s_val), axis=1, keepdims=True)
    col = lax.broadcasted_iota(jnp.int32, (live, 128), 1)
    table = jnp.where(col == 0, t_top, 1.0)
    for i, value in ((1, s_top), (2, t_sum), (3, s_sum), (4, cross)):
        table = jnp.where(col == i, value, table)
    if lanes > live:
        table = jnp.concatenate([table, jnp.ones((lanes - live, 128), jnp.float32)], axis=0)
    st[me] = jnp.transpose(table)[0:8]
    for r in range(1, n):
        go(remote(st.at[me], st.at[me], st_send.at[r], st_recv.at[me], {"dp": lax.rem(me + r, n)}))
    for r in range(1, n):
        shard = lax.rem(me + r, n)
        remote(st.at[shard], st.at[shard], st_send.at[r], st_recv.at[shard], {"dp": shard}).wait_recv()
    joined = merge(st, n)
    ones = jnp.ones((3, lanes), jnp.float32)
    sz[vi] = jnp.concatenate(list(joined) + [ones], axis=0)
    for r in range(1, nv):
        go(remote(sz.at[vi], sz.at[vi], sz_send.at[r], sz_recv.at[vi], {"vocab": lax.rem(vi + r, nv)}))
    for r in range(1, nv):
        shard = lax.rem(vi + r, nv)
        remote(sz.at[shard], sz.at[shard], sz_send.at[r], sz_recv.at[shard], {"vocab": shard}).wait_recv()
    t_top, s_top, t_sum, s_sum, cross = merge(sz, nv)
    t_norm = t_top + jnp.log(t_sum)
    s_norm = s_top + jnp.log(s_sum)
    divergence = cross / t_sum - t_norm + s_norm
    lane = lax.broadcasted_iota(jnp.int32, (1, lanes), 1)
    divergence = jnp.where(lane < live, divergence, 0.0)
    loss_ref[...] = jnp.sum(divergence, axis=1, keepdims=True) / live
    norms = jnp.concatenate([t_norm, s_norm, jnp.zeros((126, lanes), jnp.float32)], axis=0)
    norms = jnp.transpose(norms)[:live]
    gap = jnp.exp(s_val - norms[:, 1:2]) - jnp.exp(t_val - norms[:, 0:1])
    grad = (gap * (loss_scale / live)).astype(jnp.bfloat16)

    spread = tn(onehot_s[0:live, :], grad)
    sides = [
        jnp.concatenate([spread[(2 * c + k) * pair:(2 * c + k) * pair + rows] for c in range(nc)], axis=0)
        for k in range(2)
    ]
    is_zero = core == 0
    lgx[0:nc * rows] = jnp.where(is_zero, sides[1], sides[0]).astype(jnp.bfloat16)
    lgx[nc * rows:] = jnp.where(is_zero, sides[0], sides[1]).astype(jnp.bfloat16)

    half = core_out.shape[3]

    def partial(j):
        base = pl.multiple_of(lax.rem(vi + 1 + j, nv) * (2 * half), 16)
        low = nt(lgx[...], shead[pl.ds(base, half), :])
        high = nt(lgx[...], shead[pl.ds(pl.multiple_of(base + half, 16), half), :])
        blocks = [
            jnp.concatenate([low[c * rows:(c + 1) * rows], high[c * rows:(c + 1) * rows]], axis=0)
            for c in range(2 * nc)
        ]
        for c in range(nc):
            core_out[j, c] = blocks[c].astype(jnp.bfloat16)
        go(remote(core_out.at[j], core_in.at[j], c_send.at[j], c_recv.at[j], {"dp": partner}))
        for c in range(nc):
            mine[j, c] = blocks[nc + c]

    def to_plane(j):
        remote(core_out.at[j], core_in.at[j], c_send.at[j], c_recv.at[j], {"dp": partner}).wait_recv()
        mine[j] = mine[j] + core_in[j].astype(jnp.float32)
        plane_out[j] = mine[j].astype(jnp.bfloat16)
        for r in range(1, nc):
            to = lax.rem(chip + r, nc)
            go(remote(plane_out.at[j, to], plane_in.at[j, r], p_send.at[j, r], p_recv.at[j, r], {"dp": 2 * to + core}))

    for j in range(nv + 1):
        if j < nv:
            partial(j)
        if j >= 1:
            to_plane(j - 1)
    tile = 512
    slabs = ds // tile
    for j in range(nv):
        for i in range(slabs * j // nv, slabs * (j + 1) // nv):
            ghead_ref[i * tile:(i + 1) * tile, :] = tn(hc_ref[:, i * tile:(i + 1) * tile], grad).astype(jnp.bfloat16)
        total = mine[j, chip]
        for r in range(1, nc):
            remote(plane_in.at[j, r], plane_in.at[j, r], p_send.at[j, r], p_recv.at[j, r], {"dp": partner}).wait_recv()
            total = total + plane_in[j, r].astype(jnp.float32)
        if j < nv - 1:
            z_out[j] = total.astype(jnp.bfloat16)
            go(remote(z_out.at[j], z_in.at[j], z_send.at[j], z_recv.at[j], {"vocab": lax.rem(vi + 1 + j, nv)}))
        else:
            own[...] = total
    total = own[...]
    for j in range(nv - 1):
        remote(z_in.at[j], z_in.at[j], z_send.at[j], z_recv.at[j], {"vocab": lax.rem(vi + 1, nv)}).wait_recv()
        total = total + z_in[j].astype(jnp.float32)
    gh_ref[...] = jnp.concatenate([total[:rows], total[rows:]], axis=1).astype(jnp.bfloat16)
    for copy in waits:
        copy.wait_send()


def per_device(
    student_hidden,
    teacher_hidden,
    student_head,
    teacher_head,
    live_count,
    teacher_count,
    teacher_dest,
):
    rows, ds = student_hidden.shape
    dt = teacher_hidden.shape[1]
    vocab = student_head.shape[1]
    n = lax.axis_size("dp")
    nv = lax.axis_size("vocab")
    nc = n // 2
    live = rows * n // 2
    lanes = -(-live // 128) * 128
    pair = 2 * rows
    width = n * pair
    half = ds // nv // 2
    bf16, f32 = jnp.bfloat16, jnp.float32
    vmem = pl.BlockSpec(memory_space=pltpu.VMEM)
    hbm = pl.BlockSpec(memory_space=pltpu.HBM)
    dma = pltpu.SemaphoreType.DMA
    smem = pl.BlockSpec(memory_space=pltpu.SMEM)
    cuts = []
    for b, sizes in enumerate(((1024, 768), (768, 768, 768))):
        at = 0
        for size in sizes:
            cuts.append((b, at, size))
            at += size
        assert at == (ds, dt)[b] // 2
    pieces = len(cuts)
    loss, grad_head, grad_hidden = pl.pallas_call(
        functools.partial(main_kernel, n, nv, rows, live, cuts, pieces),
        out_shape=(
            jax.ShapeDtypeStruct((1, 1), f32),
            pltpu.VMEM((ds, vocab), bf16),
            pltpu.VMEM((rows, 2 * half), bf16),
        ),
        in_specs=[vmem, vmem, smem, smem, smem, hbm, hbm],
        out_specs=(vmem, vmem, vmem),
        scratch_shapes=[
            *[pltpu.VMEM((n, pair, size), bf16) for _, _, size in cuts],
            pltpu.VMEM((n, 8, width), jnp.int32),
            pltpu.VMEM((ds, vocab), bf16),
            pltpu.VMEM((dt, vocab), bf16),
            pltpu.VMEM((2 * live, width), bf16),
            pltpu.VMEM((2 * live, width), bf16),
            pltpu.VMEM((live, ds), bf16),
            pltpu.VMEM((live, vocab), f32),
            pltpu.VMEM((live, vocab), f32),
            pltpu.VMEM((n, 8, lanes), f32),
            pltpu.VMEM((nv, 8, lanes), f32),
            pltpu.VMEM((2 * nc * rows, vocab), bf16),
            pltpu.VMEM((nv, nc, pair, half), bf16),
            pltpu.VMEM((nv, nc, pair, half), bf16),
            pltpu.VMEM((nv, nc, pair, half), f32),
            pltpu.VMEM((nv, nc, pair, half), bf16),
            pltpu.VMEM((nv, nc, pair, half), bf16),
            pltpu.VMEM((pair, half), f32),
            pltpu.VMEM((nv, pair, half), bf16),
            pltpu.VMEM((nv, pair, half), bf16),
            dma((2,)),
            dma((n,)), dma((n,)),
            dma((pieces, nc)), dma((pieces, nc)), dma((pieces, n)), dma((pieces, 2)), dma((pieces, 2)),
            dma((n,)), dma((n,)), dma((nv,)), dma((nv,)),
            dma((nv,)), dma((nv,)), dma((nv, nc)), dma((nv, nc)), dma((nv,)), dma((nv,)),
        ],
        compiler_params=pltpu.CompilerParams(
            collective_id=0, has_side_effects=True, vmem_limit_bytes=(56 if n <= 8 else 58) * 2**20
        ),
        name="distill",
    )(student_hidden, teacher_hidden, live_count, teacher_count, teacher_dest, student_head, teacher_head)
    return (loss[0, 0], grad_hidden, grad_head)


def solution(mesh):
    return jax.shard_map(
        per_device,
        mesh=mesh,
        in_specs=(
            P("dp", None),
            P("dp", None),
            P(None, ("dp", "vocab")),
            P(None, ("dp", "vocab")),
            P("dp"),
            P("dp"),
            P("dp"),
        ),
        out_specs=(P(), P("dp", "vocab"), P(None, ("dp", "vocab"))),
        check_vma=False,
    )
```

```python
import functools

import jax
import jax.numpy as jnp
from jax import lax
from jax.experimental import pallas as pl
from jax.experimental.pallas import tpu as pltpu
from jax.sharding import PartitionSpec as P

loss_scale = 65536.0
MESH = pl.DeviceIdType.MESH


def nt(a, b):
    return lax.dot_general(a, b, (((1,), (1,)), ((), ())), preferred_element_type=jnp.float32)


def tn(a, b):
    return lax.dot_general(a, b, (((0,), (0,)), ((), ())), preferred_element_type=jnp.float32)


def nn(a, b):
    return jnp.dot(a, b, preferred_element_type=jnp.float32)


def merge(parts, count):
    t_top = parts[0, 0:1]
    s_top = parts[0, 1:2]
    for i in range(1, count):
        t_top = jnp.maximum(t_top, parts[i, 0:1])
        s_top = jnp.maximum(s_top, parts[i, 1:2])
    t_sum = jnp.zeros_like(t_top)
    s_sum = jnp.zeros_like(t_top)
    cross = jnp.zeros_like(t_top)
    for i in range(count):
        t_scale = jnp.exp(parts[i, 0:1] - t_top)
        t_sum += parts[i, 2:3] * t_scale
        cross += parts[i, 4:5] * t_scale
        s_sum += parts[i, 3:4] * jnp.exp(parts[i, 1:2] - s_top)
    return t_top, s_top, t_sum, s_sum, cross


def main_kernel(
    n, nv, rows, live, cuts, npieces,
    sh_ref, th_ref, live_ref, count_ref, dest_ref, shead_hbm, thead_hbm,
    loss_ref, ghead_ref, gh_ref, *scratch,
):
    bufs, scratch = scratch[:npieces], scratch[npieces:]
    (
        gm, shead, thead, onehot_s, onehot_t, hc_ref, hct, s_log, t_log,
        st, sz, lgx, core_out, core_in, mine, plane_out, plane_in, own, z_out, z_in,
        head_sem, m_send, m_recv, ici_send, core_send, g_recv, relay_send, relay_recv,
        st_send, st_recv, sz_send, sz_recv, c_send, c_recv, p_send, p_recv, z_send, z_recv,
    ) = scratch
    nc = n // 2
    me = lax.axis_index("dp")
    vi = lax.axis_index("vocab")
    core = lax.rem(me, 2)
    chip = lax.div(me, 2)
    partner = 2 * chip + 1 - core
    pair = 2 * rows
    width = n * pair
    ds, dt = shead.shape[0], thead.shape[0]

    head_copies = [
        pltpu.make_async_copy(shead_hbm, shead, head_sem.at[0]),
        pltpu.make_async_copy(thead_hbm, thead, head_sem.at[1]),
    ]
    for copy in head_copies:
        copy.start()

    barrier = pltpu.get_barrier_semaphore()
    for r in range(1, n):
        pl.semaphore_signal(barrier, inc=1, device_id={"dp": lax.rem(me + r, n)}, device_id_type=MESH)
    for r in range(1, nv):
        pl.semaphore_signal(barrier, inc=1, device_id={"vocab": lax.rem(vi + r, nv)}, device_id_type=MESH)

    def fold(i):
        b, at, size = cuts[i]
        ref = (sh_ref, th_ref)[b]
        half = ref.shape[1] // 2
        left = ref[:, at:at + size].astype(jnp.float32)
        right = ref[:, half + at:half + at + size].astype(jnp.float32)
        bufs[i][me] = jnp.concatenate([left, right], axis=0).astype(jnp.bfloat16)

    lane = lax.broadcasted_iota(jnp.int32, (1, width), 1)
    half_l = jnp.zeros((1, width), jnp.int32)
    shard_l = jnp.zeros((1, width), jnp.int32)
    pos_l = lane
    for i in range(1, 2 * n):
        pos_l = jnp.where(lane >= i * rows, lane - i * rows, pos_l)
        half_l = jnp.where(lane >= i * rows, i % 2, half_l)
        shard_l = jnp.where(lane >= i * rows, i // 2, shard_l)
    dest_l = jnp.zeros((1, width), jnp.int32)
    for i in range(rows):
        dest_l = jnp.where(pos_l == i, dest_ref[i], dest_l)
    here = shard_l == me
    gm[me] = jnp.concatenate(
        [
            jnp.where(here, live_ref[0], 0),
            jnp.where(shard_l > me, live_ref[0], 0),
            jnp.where(here, count_ref[0], 0),
            jnp.where(here, dest_l, 0),
            jnp.zeros((4, width), jnp.int32),
        ],
        axis=0,
    )
    fold(0)
    fold(1)
    pl.semaphore_wait(barrier, n - 1 + nv - 1)

    def remote(src, dst, send, recv, target):
        return pltpu.make_async_remote_copy(
            src_ref=src, dst_ref=dst, send_sem=send, recv_sem=recv,
            device_id=target, device_id_type=MESH,
        )

    waits = []

    late = []

    def go(copy, kept=waits):
        copy.start()
        kept.append(copy)

    square = nc == 4
    x_chip = 2 * lax.div(chip, 2) + 1 - lax.rem(chip, 2)
    y_chip = lax.rem(chip + 2, 4)
    targets = [x_chip, y_chip] if square else [lax.rem(chip + r, nc) for r in range(1, nc)]
    sources = [x_chip, y_chip] if square else [lax.rem(chip + nc - r, nc) for r in range(1, nc)]

    def block_copy(i, shard, send, target):
        return remote(bufs[i].at[shard], bufs[i].at[shard], send, g_recv.at[i, shard], {"dp": target})

    def start_own(i):
        for r, to in enumerate(targets):
            go(block_copy(i, me, ici_send.at[i, r], 2 * to + core))
        go(block_copy(i, me, core_send.at[i, 0], partner))

    def pass_on(i):
        for r, source in enumerate(sources):
            shard = 2 * source + core
            block_copy(i, shard, core_send.at[i, r + 1], partner).wait_recv()
            if square:
                size = bufs[i].shape[2] // 2
                to = (y_chip, x_chip)[r]
                part = bufs[i].at[shard, :, pl.ds(r * size, size)]
                go(remote(part, part, relay_send.at[i, r], relay_recv.at[i, r], {"dp": 2 * to + core}))
            go(block_copy(i, shard, core_send.at[i, r + 1], partner))

    def finish(i):
        if square:
            shard = 2 * (3 - chip) + core
            for r in range(2):
                size = bufs[i].shape[2] // 2
                part = bufs[i].at[shard, :, pl.ds(r * size, size)]
                remote(part, part, relay_send.at[i, r], relay_recv.at[i, r], {"dp": partner}).wait_recv()
            go(block_copy(i, shard, core_send.at[i, 3], partner))
        for c in range(nc):
            block_copy(i, 2 * c + 1 - core, core_send.at[i, 0], partner).wait_recv()

    for r in range(1, n):
        target = lax.rem(me + r, n)
        go(remote(gm.at[me], gm.at[me], m_send.at[r], m_recv.at[me], {"dp": target}))
    start_own(0)
    start_own(1)
    for i in range(2, npieces):
        fold(i)
    pass_on(0)
    start_own(2)
    for r in range(1, n):
        shard = lax.rem(me + r, n)
        remote(gm.at[shard], gm.at[shard], m_send.at[r], m_recv.at[shard], {"dp": shard}).wait_recv()
    meta = gm[0]
    for i in range(1, n):
        meta = meta + gm[i]
    live_l, off_l, count_l, dest_l = meta[0:1], meta[1:2], meta[2:3], meta[3:4]

    rank_l = jnp.zeros((1, width), jnp.int32)
    for i in range(n):
        off_i = off_l[:, i * pair:i * pair + 1]
        inside = (dest_l >= i * rows) & (dest_l < (i + 1) * rows)
        rank_l = jnp.where(inside, dest_l - i * rows + off_i, rank_l)
    shape = (2 * live, width)
    row = lax.broadcasted_iota(jnp.int32, shape, 0)
    key_s = jnp.where(pos_l < live_l, pos_l + off_l + live * half_l, -1)
    key_t = jnp.where(pos_l < count_l, rank_l + live * half_l, -1)
    onehot_s[...] = jnp.where(row == key_s, 1.0, 0.0).astype(jnp.bfloat16)
    onehot_t[...] = jnp.where(row == key_t, 1.0, 0.0).astype(jnp.bfloat16)

    def logits(i):
        b, at, size = cuts[i]
        onehot, head, out = ((onehot_s, shead, s_log), (onehot_t, thead, t_log))[b]
        half = head.shape[0] // 2
        packed = nn(onehot[...], bufs[i][...].reshape(width, size)).astype(jnp.bfloat16)
        top, low = packed[:live], packed[live:]
        if b == 0:
            hc_ref[:, at:at + size] = top
            hc_ref[:, half + at:half + at + size] = low
        value = nn(top, head[at:at + size, :]) + nn(low, head[half + at:half + at + size, :])
        out[...] = value if at == 0 else out[...] + value

    for i in range(npieces + 1):
        if 0 < i < npieces:
            pass_on(i)
            if i + 2 < npieces:
                start_own(i + 2)
        if i >= 1:
            finish(i - 1)
            b, at, _ = cuts[i - 1]
            if at == 0:
                head_copies[b].wait()
            logits(i - 1)

    lanes = st.shape[2]
    s_val, t_val = s_log[...], t_log[...]
    t_top = jnp.max(t_val, axis=1, keepdims=True)
    s_top = jnp.max(s_val, axis=1, keepdims=True)
    t_exp = jnp.exp(t_val - t_top)
    t_sum = jnp.sum(t_exp, axis=1, keepdims=True)
    s_sum = jnp.sum(jnp.exp(s_val - s_top), axis=1, keepdims=True)
    cross = jnp.sum(t_exp * (t_val - s_val), axis=1, keepdims=True)
    col = lax.broadcasted_iota(jnp.int32, (live, 128), 1)
    table = jnp.where(col == 0, t_top, 1.0)
    for i, value in ((1, s_top), (2, t_sum), (3, s_sum), (4, cross)):
        table = jnp.where(col == i, value, table)
    if lanes > live:
        table = jnp.concatenate([table, jnp.ones((lanes - live, 128), jnp.float32)], axis=0)
    st[me] = jnp.transpose(table)[0:8]
    for r in range(1, n):
        go(remote(st.at[me], st.at[me], st_send.at[r], st_recv.at[me], {"dp": lax.rem(me + r, n)}))
    tile = 512
    slabs = ds // tile

    def turn(first, last):
        for i in range(first, last):
            hct[i * tile:(i + 1) * tile, :] = jnp.transpose(hc_ref[:, i * tile:(i + 1) * tile])

    turn(0, slabs // 2)
    for r in range(1, n):
        shard = lax.rem(me + r, n)
        remote(st.at[shard], st.at[shard], st_send.at[r], st_recv.at[shard], {"dp": shard}).wait_recv()
    joined = merge(st, n)
    ones = jnp.ones((3, lanes), jnp.float32)
    sz[vi] = jnp.concatenate(list(joined) + [ones], axis=0)
    for r in range(1, nv):
        go(remote(sz.at[vi], sz.at[vi], sz_send.at[r], sz_recv.at[vi], {"vocab": lax.rem(vi + r, nv)}))
    turn(slabs // 2, slabs)
    for r in range(1, nv):
        shard = lax.rem(vi + r, nv)
        remote(sz.at[shard], sz.at[shard], sz_send.at[r], sz_recv.at[shard], {"vocab": shard}).wait_recv()
    t_top, s_top, t_sum, s_sum, cross = merge(sz, nv)
    t_norm = t_top + jnp.log(t_sum)
    s_norm = s_top + jnp.log(s_sum)
    divergence = cross / t_sum - t_norm + s_norm
    lane = lax.broadcasted_iota(jnp.int32, (1, lanes), 1)
    divergence = jnp.where(lane < live, divergence, 0.0)
    loss_ref[...] = jnp.sum(divergence, axis=1, keepdims=True) / live
    norms = jnp.concatenate([t_norm, s_norm, jnp.zeros((126, lanes), jnp.float32)], axis=0)
    norms = jnp.transpose(norms)[:live]
    gap = jnp.exp(s_val - norms[:, 1:2]) - jnp.exp(t_val - norms[:, 0:1])
    grad = (gap * (loss_scale / live)).astype(jnp.bfloat16)

    spread = tn(onehot_s[0:live, :], grad)
    sides = [
        jnp.concatenate([spread[(2 * c + k) * pair:(2 * c + k) * pair + rows] for c in range(nc)], axis=0)
        for k in range(2)
    ]
    is_zero = core == 0
    lgx[0:nc * rows] = jnp.where(is_zero, sides[1], sides[0]).astype(jnp.bfloat16)
    lgx[nc * rows:] = jnp.where(is_zero, sides[0], sides[1]).astype(jnp.bfloat16)

    half = core_out.shape[3]

    def partial(j):
        base = pl.multiple_of(lax.rem(vi + 1 + j, nv) * (2 * half), 16)
        low = nt(lgx[...], shead[pl.ds(base, half), :])
        high = nt(lgx[...], shead[pl.ds(pl.multiple_of(base + half, 16), half), :])
        blocks = [
            jnp.concatenate([low[c * rows:(c + 1) * rows], high[c * rows:(c + 1) * rows]], axis=0)
            for c in range(2 * nc)
        ]
        for c in range(nc):
            core_out[j, c] = blocks[c].astype(jnp.bfloat16)
        go(remote(core_out.at[j], core_in.at[j], c_send.at[j], c_recv.at[j], {"dp": partner}))
        for c in range(nc):
            mine[j, c] = blocks[nc + c]

    def to_plane(j):
        remote(core_out.at[j], core_in.at[j], c_send.at[j], c_recv.at[j], {"dp": partner}).wait_recv()
        mine[j] = mine[j] + core_in[j].astype(jnp.float32)
        plane_out[j] = mine[j].astype(jnp.bfloat16)
        for r in range(1, nc):
            to = lax.rem(chip + r, nc)
            go(remote(plane_out.at[j, to], plane_in.at[j, r], p_send.at[j, r], p_recv.at[j, r], {"dp": 2 * to + core}), late)

    for j in range(nv + 1):
        if j < nv:
            partial(j)
        if j >= 1:
            to_plane(j - 1)
    for j in range(nv):
        for i in range(slabs * j // nv, slabs * (j + 1) // nv):
            ghead_ref[i * tile:(i + 1) * tile, :] = nn(hct[i * tile:(i + 1) * tile, :], grad).astype(jnp.bfloat16)
        if j == 0:
            for copy in waits:
                copy.wait_send()
        total = mine[j, chip]
        for r in range(1, nc):
            remote(plane_in.at[j, r], plane_in.at[j, r], p_send.at[j, r], p_recv.at[j, r], {"dp": partner}).wait_recv()
            total = total + plane_in[j, r].astype(jnp.float32)
        if j < nv - 1:
            z_out[j] = total.astype(jnp.bfloat16)
            go(remote(z_out.at[j], z_in.at[j], z_send.at[j], z_recv.at[j], {"vocab": lax.rem(vi + 1 + j, nv)}), late)
        else:
            own[...] = total
    total = own[...]
    for j in range(nv - 1):
        remote(z_in.at[j], z_in.at[j], z_send.at[j], z_recv.at[j], {"vocab": lax.rem(vi + 1, nv)}).wait_recv()
        total = total + z_in[j].astype(jnp.float32)
    gh_ref[...] = jnp.concatenate([total[:rows], total[rows:]], axis=1).astype(jnp.bfloat16)
    for copy in late:
        copy.wait_send()


def per_device(
    student_hidden,
    teacher_hidden,
    student_head,
    teacher_head,
    live_count,
    teacher_count,
    teacher_dest,
):
    rows, ds = student_hidden.shape
    dt = teacher_hidden.shape[1]
    vocab = student_head.shape[1]
    n = lax.axis_size("dp")
    nv = lax.axis_size("vocab")
    nc = n // 2
    live = rows * n // 2
    lanes = -(-live // 128) * 128
    pair = 2 * rows
    width = n * pair
    half = ds // nv // 2
    bf16, f32 = jnp.bfloat16, jnp.float32
    vmem = pl.BlockSpec(memory_space=pltpu.VMEM)
    hbm = pl.BlockSpec(memory_space=pltpu.HBM)
    dma = pltpu.SemaphoreType.DMA
    smem = pl.BlockSpec(memory_space=pltpu.SMEM)
    cuts = []
    for b, sizes in enumerate(((1024, 768), (768, 768, 768))):
        at = 0
        for size in sizes:
            cuts.append((b, at, size))
            at += size
        assert at == (ds, dt)[b] // 2
    pieces = len(cuts)
    loss, grad_head, grad_hidden = pl.pallas_call(
        functools.partial(main_kernel, n, nv, rows, live, cuts, pieces),
        out_shape=(
            jax.ShapeDtypeStruct((1, 1), f32),
            pltpu.VMEM((ds, vocab), bf16),
            pltpu.VMEM((rows, 2 * half), bf16),
        ),
        in_specs=[vmem, vmem, smem, smem, smem, hbm, hbm],
        out_specs=(vmem, vmem, vmem),
        scratch_shapes=[
            *[pltpu.VMEM((n, pair, size), bf16) for _, _, size in cuts],
            pltpu.VMEM((n, 8, width), jnp.int32),
            pltpu.VMEM((ds, vocab), bf16),
            pltpu.VMEM((dt, vocab), bf16),
            pltpu.VMEM((2 * live, width), bf16),
            pltpu.VMEM((2 * live, width), bf16),
            pltpu.VMEM((live, ds), bf16),
            pltpu.VMEM((ds, live), bf16),
            pltpu.VMEM((live, vocab), f32),
            pltpu.VMEM((live, vocab), f32),
            pltpu.VMEM((n, 8, lanes), f32),
            pltpu.VMEM((nv, 8, lanes), f32),
            pltpu.VMEM((2 * nc * rows, vocab), bf16),
            pltpu.VMEM((nv, nc, pair, half), bf16),
            pltpu.VMEM((nv, nc, pair, half), bf16),
            pltpu.VMEM((nv, nc, pair, half), f32),
            pltpu.VMEM((nv, nc, pair, half), bf16),
            pltpu.VMEM((nv, nc, pair, half), bf16),
            pltpu.VMEM((pair, half), f32),
            pltpu.VMEM((nv, pair, half), bf16),
            pltpu.VMEM((nv, pair, half), bf16),
            dma((2,)),
            dma((n,)), dma((n,)),
            dma((pieces, nc)), dma((pieces, nc)), dma((pieces, n)), dma((pieces, 2)), dma((pieces, 2)),
            dma((n,)), dma((n,)), dma((nv,)), dma((nv,)),
            dma((nv,)), dma((nv,)), dma((nv, nc)), dma((nv, nc)), dma((nv,)), dma((nv,)),
        ],
        compiler_params=pltpu.CompilerParams(
            collective_id=0, has_side_effects=True, vmem_limit_bytes=(56 if n <= 8 else 58) * 2**20
        ),
        name="distill",
    )(student_hidden, teacher_hidden, live_count, teacher_count, teacher_dest, student_head, teacher_head)
    return (loss[0, 0], grad_hidden, grad_head)


def solution(mesh):
    return jax.shard_map(
        per_device,
        mesh=mesh,
        in_specs=(
            P("dp", None),
            P("dp", None),
            P(None, ("dp", "vocab")),
            P(None, ("dp", "vocab")),
            P("dp"),
            P("dp"),
            P("dp"),
        ),
        out_specs=(P(), P("dp", "vocab"), P(None, ("dp", "vocab"))),
        check_vma=False,
    )
```

```python
import functools

import jax
import jax.numpy as jnp
from jax import lax
from jax.experimental import pallas as pl
from jax.experimental.pallas import tpu as pltpu
from jax.sharding import PartitionSpec as P

loss_scale = 65536.0
MESH = pl.DeviceIdType.MESH


def nt(a, b):
    return lax.dot_general(a, b, (((1,), (1,)), ((), ())), preferred_element_type=jnp.float32)


def tn(a, b):
    return lax.dot_general(a, b, (((0,), (0,)), ((), ())), preferred_element_type=jnp.float32)


def nn(a, b):
    return jnp.dot(a, b, preferred_element_type=jnp.float32)


def merge(parts, count):
    t_top = parts[0, 0:1]
    s_top = parts[0, 1:2]
    for i in range(1, count):
        t_top = jnp.maximum(t_top, parts[i, 0:1])
        s_top = jnp.maximum(s_top, parts[i, 1:2])
    t_sum = jnp.zeros_like(t_top)
    s_sum = jnp.zeros_like(t_top)
    cross = jnp.zeros_like(t_top)
    for i in range(count):
        t_scale = jnp.exp(parts[i, 0:1] - t_top)
        t_sum += parts[i, 2:3] * t_scale
        cross += parts[i, 4:5] * t_scale
        s_sum += parts[i, 3:4] * jnp.exp(parts[i, 1:2] - s_top)
    return t_top, s_top, t_sum, s_sum, cross


def main_kernel(
    n, nv, rows, live, cuts, npieces,
    sh_ref, th_ref, live_ref, count_ref, dest_ref, shead_hbm, thead_hbm,
    loss_ref, ghead_ref, gh_ref, *scratch,
):
    bufs, scratch = scratch[:npieces], scratch[npieces:]
    (
        gm, shead, thead, onehot_s, onehot_t, hc_ref, hct, s_log, t_log,
        st, sz, lgx, core_out, core_in, mine, plane_out, plane_in, own, z_out, z_in,
        head_sem, m_send, m_recv, ici_send, core_send, g_recv, hop_send, hop_recv,
        st_send, st_recv, sz_send, sz_recv, c_send, c_recv, p_send, p_recv, z_send, z_recv,
    ) = scratch
    nc = n // 2
    me = lax.axis_index("dp")
    vi = lax.axis_index("vocab")
    core = lax.rem(me, 2)
    chip = lax.div(me, 2)
    partner = 2 * chip + 1 - core
    pair = 2 * rows
    width = n * pair
    ds, dt = shead.shape[0], thead.shape[0]

    head_copies = [
        pltpu.make_async_copy(shead_hbm, shead, head_sem.at[0]),
        pltpu.make_async_copy(thead_hbm, thead, head_sem.at[1]),
    ]
    for copy in head_copies:
        copy.start()

    barrier = pltpu.get_barrier_semaphore()
    for r in range(1, n):
        pl.semaphore_signal(barrier, inc=1, device_id={"dp": lax.rem(me + r, n)}, device_id_type=MESH)
    for r in range(1, nv):
        pl.semaphore_signal(barrier, inc=1, device_id={"vocab": lax.rem(vi + r, nv)}, device_id_type=MESH)

    def fold(i):
        b, at, size = cuts[i]
        ref = (sh_ref, th_ref)[b]
        half = ref.shape[1] // 2
        left = ref[:, at:at + size].astype(jnp.float32)
        right = ref[:, half + at:half + at + size].astype(jnp.float32)
        bufs[i][me] = jnp.concatenate([left, right], axis=0).astype(jnp.bfloat16)

    lane = lax.broadcasted_iota(jnp.int32, (1, width), 1)
    half_l = jnp.zeros((1, width), jnp.int32)
    shard_l = jnp.zeros((1, width), jnp.int32)
    pos_l = lane
    for i in range(1, 2 * n):
        pos_l = jnp.where(lane >= i * rows, lane - i * rows, pos_l)
        half_l = jnp.where(lane >= i * rows, i % 2, half_l)
        shard_l = jnp.where(lane >= i * rows, i // 2, shard_l)
    dest_l = jnp.zeros((1, width), jnp.int32)
    for i in range(rows):
        dest_l = jnp.where(pos_l == i, dest_ref[i], dest_l)
    here = shard_l == me
    gm[me] = jnp.concatenate(
        [
            jnp.where(here, live_ref[0], 0),
            jnp.where(shard_l > me, live_ref[0], 0),
            jnp.where(here, count_ref[0], 0),
            jnp.where(here, dest_l, 0),
            jnp.zeros((4, width), jnp.int32),
        ],
        axis=0,
    )
    fold(0)
    fold(1)
    pl.semaphore_wait(barrier, n - 1 + nv - 1)

    def remote(src, dst, send, recv, target):
        return pltpu.make_async_remote_copy(
            src_ref=src, dst_ref=dst, send_sem=send, recv_sem=recv,
            device_id=target, device_id_type=MESH,
        )

    waits = []

    late = []

    def go(copy, kept=waits):
        copy.start()
        kept.append(copy)

    square = nc == 4 and nv % 2 == 0
    even = lax.rem(vi, 2)
    z_pair = vi + 1 - 2 * even
    x_chip = 2 * lax.div(chip, 2) + 1 - lax.rem(chip, 2)
    y_chip = lax.rem(chip + 2, 4)
    targets = [x_chip, y_chip] if square else [lax.rem(chip + r, nc) for r in range(1, nc)]
    sources = [x_chip, y_chip] if square else [lax.rem(chip + nc - r, nc) for r in range(1, nc)]

    def block_copy(i, shard, send, target):
        return remote(bufs[i].at[shard], bufs[i].at[shard], send, g_recv.at[i, shard], {"dp": target})

    def columns(i, shard, first, size):
        return bufs[i].at[shard, :, pl.ds(pl.multiple_of(first * 128, 128), size * 128)]

    def quarters(i):
        units = bufs[i].shape[2] // 128
        shared = units // 4
        return (units - 2 * shared) // 2, shared

    def hop(i, shard, first, size, slot, target):
        part = columns(i, shard, first, size)
        return remote(part, part, hop_send.at[i, slot], hop_recv.at[i, slot], target)

    def start_own(i):
        if square:
            plain, shared = quarters(i)
            for r, to in enumerate(targets):
                target = {"dp": 2 * to + core}
                go(hop(i, me, 0, 2 * plain, r, target))
                go(hop(i, me, 2 * plain + even * shared, shared, 2 + r, target))
        else:
            for r, to in enumerate(targets):
                go(block_copy(i, me, ici_send.at[i, r], 2 * to + core))
        go(block_copy(i, me, core_send.at[i, 0], partner))

    def pass_on(i):
        for r, source in enumerate(sources):
            shard = 2 * source + core
            if square:
                plain, shared = quarters(i)
                mate = {"dp": 2 * (y_chip, x_chip)[r] + core}
                half_at = 2 * plain + even * shared
                hop(i, shard, 0, 2 * plain, r, mate).wait_recv()
                if r == 0:
                    go(hop(i, shard, even * plain, plain, 6, mate))
                hop(i, shard, half_at, shared, 2 + r, mate).wait_recv()
                if r == 1:
                    go(hop(i, shard, half_at, shared, 7, mate))
                go(hop(i, shard, half_at, shared, 4 + r, {"vocab": z_pair}))
            else:
                block_copy(i, shard, core_send.at[i, r + 1], partner).wait_recv()
                go(block_copy(i, shard, core_send.at[i, r + 1], partner))

    def swap(i):
        if square:
            plain, shared = quarters(i)
            mate = {"vocab": z_pair}
            shard = 2 * (3 - chip) + core
            odd = 1 - even
            hop(i, shard, even * plain, plain, 6, mate).wait_recv()
            go(hop(i, shard, even * plain, plain, 8, mate))
            hop(i, shard, 2 * plain + even * shared, shared, 7, mate).wait_recv()
            go(hop(i, shard, 2 * plain + even * shared, shared, 9, mate))
            for r, source in enumerate(sources):
                other = 2 * source + core
                hop(i, other, 2 * plain + odd * shared, shared, 4 + r, mate).wait_recv()
                go(block_copy(i, other, core_send.at[i, r + 1], partner))

    def finish(i):
        if square:
            plain, shared = quarters(i)
            mate = {"vocab": z_pair}
            shard = 2 * (3 - chip) + core
            odd = 1 - even
            hop(i, shard, odd * plain, plain, 8, mate).wait_recv()
            hop(i, shard, 2 * plain + odd * shared, shared, 9, mate).wait_recv()
            go(block_copy(i, shard, core_send.at[i, 3], partner))
        for c in range(nc):
            block_copy(i, 2 * c + 1 - core, core_send.at[i, 0], partner).wait_recv()

    for r in range(1, n):
        target = lax.rem(me + r, n)
        go(remote(gm.at[me], gm.at[me], m_send.at[r], m_recv.at[me], {"dp": target}))
    start_own(0)
    start_own(1)
    for i in range(2, npieces):
        fold(i)
    pass_on(0)
    start_own(2)
    for r in range(1, n):
        shard = lax.rem(me + r, n)
        remote(gm.at[shard], gm.at[shard], m_send.at[r], m_recv.at[shard], {"dp": shard}).wait_recv()
    meta = gm[0]
    for i in range(1, n):
        meta = meta + gm[i]
    live_l, off_l, count_l, dest_l = meta[0:1], meta[1:2], meta[2:3], meta[3:4]

    rank_l = jnp.zeros((1, width), jnp.int32)
    for i in range(n):
        off_i = off_l[:, i * pair:i * pair + 1]
        inside = (dest_l >= i * rows) & (dest_l < (i + 1) * rows)
        rank_l = jnp.where(inside, dest_l - i * rows + off_i, rank_l)
    shape = (2 * live, width)
    row = lax.broadcasted_iota(jnp.int32, shape, 0)
    key_s = jnp.where(pos_l < live_l, pos_l + off_l + live * half_l, -1)
    key_t = jnp.where(pos_l < count_l, rank_l + live * half_l, -1)
    onehot_s[...] = jnp.where(row == key_s, 1.0, 0.0).astype(jnp.bfloat16)
    onehot_t[...] = jnp.where(row == key_t, 1.0, 0.0).astype(jnp.bfloat16)

    def logits(i):
        b, at, size = cuts[i]
        onehot, head, out = ((onehot_s, shead, s_log), (onehot_t, thead, t_log))[b]
        half = head.shape[0] // 2
        packed = nn(onehot[...], bufs[i][...].reshape(width, size)).astype(jnp.bfloat16)
        top, low = packed[:live], packed[live:]
        if b == 0:
            hc_ref[:, at:at + size] = top
            hc_ref[:, half + at:half + at + size] = low
        value = nn(top, head[at:at + size, :]) + nn(low, head[half + at:half + at + size, :])
        out[...] = value if at == 0 else out[...] + value

    for i in range(npieces + 2):
        if 0 < i < npieces:
            pass_on(i)
            if i + 2 < npieces:
                start_own(i + 2)
        if 1 <= i <= npieces:
            swap(i - 1)
        if i >= 2:
            finish(i - 2)
            b, at, _ = cuts[i - 2]
            if at == 0:
                head_copies[b].wait()
            logits(i - 2)

    lanes = st.shape[2]
    s_val, t_val = s_log[...], t_log[...]
    t_top = jnp.max(t_val, axis=1, keepdims=True)
    s_top = jnp.max(s_val, axis=1, keepdims=True)
    t_exp = jnp.exp(t_val - t_top)
    t_sum = jnp.sum(t_exp, axis=1, keepdims=True)
    s_sum = jnp.sum(jnp.exp(s_val - s_top), axis=1, keepdims=True)
    cross = jnp.sum(t_exp * (t_val - s_val), axis=1, keepdims=True)
    col = lax.broadcasted_iota(jnp.int32, (live, 128), 1)
    table = jnp.where(col == 0, t_top, 1.0)
    for i, value in ((1, s_top), (2, t_sum), (3, s_sum), (4, cross)):
        table = jnp.where(col == i, value, table)
    if lanes > live:
        table = jnp.concatenate([table, jnp.ones((lanes - live, 128), jnp.float32)], axis=0)
    st[me] = jnp.transpose(table)[0:8]
    for r in range(1, n):
        go(remote(st.at[me], st.at[me], st_send.at[r], st_recv.at[me], {"dp": lax.rem(me + r, n)}))
    tile = 512
    slabs = ds // tile

    def turn(first, last):
        for i in range(first, last):
            hct[i * tile:(i + 1) * tile, :] = jnp.transpose(hc_ref[:, i * tile:(i + 1) * tile])

    turn(0, slabs // 2)
    for r in range(1, n):
        shard = lax.rem(me + r, n)
        remote(st.at[shard], st.at[shard], st_send.at[r], st_recv.at[shard], {"dp": shard}).wait_recv()
    joined = merge(st, n)
    ones = jnp.ones((3, lanes), jnp.float32)
    sz[vi] = jnp.concatenate(list(joined) + [ones], axis=0)
    for r in range(1, nv):
        go(remote(sz.at[vi], sz.at[vi], sz_send.at[r], sz_recv.at[vi], {"vocab": lax.rem(vi + r, nv)}))
    turn(slabs // 2, slabs)
    for r in range(1, nv):
        shard = lax.rem(vi + r, nv)
        remote(sz.at[shard], sz.at[shard], sz_send.at[r], sz_recv.at[shard], {"vocab": shard}).wait_recv()
    t_top, s_top, t_sum, s_sum, cross = merge(sz, nv)
    t_norm = t_top + jnp.log(t_sum)
    s_norm = s_top + jnp.log(s_sum)
    divergence = cross / t_sum - t_norm + s_norm
    lane = lax.broadcasted_iota(jnp.int32, (1, lanes), 1)
    divergence = jnp.where(lane < live, divergence, 0.0)
    loss_ref[...] = jnp.sum(divergence, axis=1, keepdims=True) / live
    norms = jnp.concatenate([t_norm, s_norm, jnp.zeros((126, lanes), jnp.float32)], axis=0)
    norms = jnp.transpose(norms)[:live]
    gap = jnp.exp(s_val - norms[:, 1:2]) - jnp.exp(t_val - norms[:, 0:1])
    grad = (gap * (loss_scale / live)).astype(jnp.bfloat16)

    spread = tn(onehot_s[0:live, :], grad)
    sides = [
        jnp.concatenate([spread[(2 * c + k) * pair:(2 * c + k) * pair + rows] for c in range(nc)], axis=0)
        for k in range(2)
    ]
    is_zero = core == 0
    lgx[0:nc * rows] = jnp.where(is_zero, sides[1], sides[0]).astype(jnp.bfloat16)
    lgx[nc * rows:] = jnp.where(is_zero, sides[0], sides[1]).astype(jnp.bfloat16)

    half = core_out.shape[3]

    def partial(j):
        base = pl.multiple_of(lax.rem(vi + 1 + j, nv) * (2 * half), 16)
        low = nt(lgx[...], shead[pl.ds(base, half), :])
        high = nt(lgx[...], shead[pl.ds(pl.multiple_of(base + half, 16), half), :])
        blocks = [
            jnp.concatenate([low[c * rows:(c + 1) * rows], high[c * rows:(c + 1) * rows]], axis=0)
            for c in range(2 * nc)
        ]
        for c in range(nc):
            core_out[j, c] = blocks[c].astype(jnp.bfloat16)
        go(remote(core_out.at[j], core_in.at[j], c_send.at[j], c_recv.at[j], {"dp": partner}))
        for c in range(nc):
            mine[j, c] = blocks[nc + c]

    def to_plane(j):
        remote(core_out.at[j], core_in.at[j], c_send.at[j], c_recv.at[j], {"dp": partner}).wait_recv()
        mine[j] = mine[j] + core_in[j].astype(jnp.float32)
        plane_out[j] = mine[j].astype(jnp.bfloat16)
        for r in range(1, nc):
            to = lax.rem(chip + r, nc)
            go(remote(plane_out.at[j, to], plane_in.at[j, r], p_send.at[j, r], p_recv.at[j, r], {"dp": 2 * to + core}), late)

    for j in range(nv + 1):
        if j < nv:
            partial(j)
        if j >= 1:
            to_plane(j - 1)
    for j in range(nv):
        for i in range(slabs * j // nv, slabs * (j + 1) // nv):
            ghead_ref[i * tile:(i + 1) * tile, :] = nn(hct[i * tile:(i + 1) * tile, :], grad).astype(jnp.bfloat16)
        if j == 0:
            for copy in waits:
                copy.wait_send()
        total = mine[j, chip]
        for r in range(1, nc):
            remote(plane_in.at[j, r], plane_in.at[j, r], p_send.at[j, r], p_recv.at[j, r], {"dp": partner}).wait_recv()
            total = total + plane_in[j, r].astype(jnp.float32)
        if j < nv - 1:
            z_out[j] = total.astype(jnp.bfloat16)
            go(remote(z_out.at[j], z_in.at[j], z_send.at[j], z_recv.at[j], {"vocab": lax.rem(vi + 1 + j, nv)}), late)
        else:
            own[...] = total
    total = own[...]
    for j in range(nv - 1):
        remote(z_in.at[j], z_in.at[j], z_send.at[j], z_recv.at[j], {"vocab": lax.rem(vi + 1, nv)}).wait_recv()
        total = total + z_in[j].astype(jnp.float32)
    gh_ref[...] = jnp.concatenate([total[:rows], total[rows:]], axis=1).astype(jnp.bfloat16)
    for copy in late:
        copy.wait_send()


def per_device(
    student_hidden,
    teacher_hidden,
    student_head,
    teacher_head,
    live_count,
    teacher_count,
    teacher_dest,
):
    rows, ds = student_hidden.shape
    dt = teacher_hidden.shape[1]
    vocab = student_head.shape[1]
    n = lax.axis_size("dp")
    nv = lax.axis_size("vocab")
    nc = n // 2
    live = rows * n // 2
    lanes = -(-live // 128) * 128
    pair = 2 * rows
    width = n * pair
    half = ds // nv // 2
    bf16, f32 = jnp.bfloat16, jnp.float32
    vmem = pl.BlockSpec(memory_space=pltpu.VMEM)
    hbm = pl.BlockSpec(memory_space=pltpu.HBM)
    dma = pltpu.SemaphoreType.DMA
    smem = pl.BlockSpec(memory_space=pltpu.SMEM)
    cuts = []
    for b, sizes in enumerate(((1024, 768), (1024, 768, 512))):
        at = 0
        for size in sizes:
            cuts.append((b, at, size))
            at += size
        assert at == (ds, dt)[b] // 2
    pieces = len(cuts)
    loss, grad_head, grad_hidden = pl.pallas_call(
        functools.partial(main_kernel, n, nv, rows, live, cuts, pieces),
        out_shape=(
            jax.ShapeDtypeStruct((1, 1), f32),
            pltpu.VMEM((ds, vocab), bf16),
            pltpu.VMEM((rows, 2 * half), bf16),
        ),
        in_specs=[vmem, vmem, smem, smem, smem, hbm, hbm],
        out_specs=(vmem, vmem, vmem),
        scratch_shapes=[
            *[pltpu.VMEM((n, pair, size), bf16) for _, _, size in cuts],
            pltpu.VMEM((n, 8, width), jnp.int32),
            pltpu.VMEM((ds, vocab), bf16),
            pltpu.VMEM((dt, vocab), bf16),
            pltpu.VMEM((2 * live, width), bf16),
            pltpu.VMEM((2 * live, width), bf16),
            pltpu.VMEM((live, ds), bf16),
            pltpu.VMEM((ds, live), bf16),
            pltpu.VMEM((live, vocab), f32),
            pltpu.VMEM((live, vocab), f32),
            pltpu.VMEM((n, 8, lanes), f32),
            pltpu.VMEM((nv, 8, lanes), f32),
            pltpu.VMEM((2 * nc * rows, vocab), bf16),
            pltpu.VMEM((nv, nc, pair, half), bf16),
            pltpu.VMEM((nv, nc, pair, half), bf16),
            pltpu.VMEM((nv, nc, pair, half), f32),
            pltpu.VMEM((nv, nc, pair, half), bf16),
            pltpu.VMEM((nv, nc, pair, half), bf16),
            pltpu.VMEM((pair, half), f32),
            pltpu.VMEM((nv, pair, half), bf16),
            pltpu.VMEM((nv, pair, half), bf16),
            dma((2,)),
            dma((n,)), dma((n,)),
            dma((pieces, nc)), dma((pieces, nc)), dma((pieces, n)), dma((pieces, 10)), dma((pieces, 10)),
            dma((n,)), dma((n,)), dma((nv,)), dma((nv,)),
            dma((nv,)), dma((nv,)), dma((nv, nc)), dma((nv, nc)), dma((nv,)), dma((nv,)),
        ],
        compiler_params=pltpu.CompilerParams(
            collective_id=0, has_side_effects=True, vmem_limit_bytes=(56 if n <= 8 else 58) * 2**20
        ),
        name="distill",
    )(student_hidden, teacher_hidden, live_count, teacher_count, teacher_dest, student_head, teacher_head)
    return (loss[0, 0], grad_hidden, grad_head)


def solution(mesh):
    return jax.shard_map(
        per_device,
        mesh=mesh,
        in_specs=(
            P("dp", None),
            P("dp", None),
            P(None, ("dp", "vocab")),
            P(None, ("dp", "vocab")),
            P("dp"),
            P("dp"),
            P("dp"),
        ),
        out_specs=(P(), P("dp", "vocab"), P(None, ("dp", "vocab"))),
        check_vma=False,
    )
```

```python
import functools

import jax
import jax.numpy as jnp
from jax import lax
from jax.experimental import pallas as pl
from jax.experimental.pallas import tpu as pltpu
from jax.sharding import PartitionSpec as P

loss_scale = 65536.0
MESH = pl.DeviceIdType.MESH


def nt(a, b):
    return lax.dot_general(a, b, (((1,), (1,)), ((), ())), preferred_element_type=jnp.float32)


def tn(a, b):
    return lax.dot_general(a, b, (((0,), (0,)), ((), ())), preferred_element_type=jnp.float32)


def nn(a, b):
    return jnp.dot(a, b, preferred_element_type=jnp.float32)


def merge(parts, count):
    t_top = parts[0, 0:1]
    s_top = parts[0, 1:2]
    for i in range(1, count):
        t_top = jnp.maximum(t_top, parts[i, 0:1])
        s_top = jnp.maximum(s_top, parts[i, 1:2])
    t_sum = jnp.zeros_like(t_top)
    s_sum = jnp.zeros_like(t_top)
    cross = jnp.zeros_like(t_top)
    for i in range(count):
        t_scale = jnp.exp(parts[i, 0:1] - t_top)
        t_sum += parts[i, 2:3] * t_scale
        cross += parts[i, 4:5] * t_scale
        s_sum += parts[i, 3:4] * jnp.exp(parts[i, 1:2] - s_top)
    return t_top, s_top, t_sum, s_sum, cross


def main_kernel(
    n, nv, rows, live, cuts, npieces,
    sh_ref, th_ref, live_ref, count_ref, dest_ref, shead_hbm, thead_hbm,
    loss_ref, ghead_ref, gh_ref, *scratch,
):
    bufs, scratch = scratch[:npieces], scratch[npieces:]
    (
        gm, shead, thead, onehot_s, onehot_t, hc_ref, hct, s_log, t_log,
        st, sz, lgx, core_out, core_in, mine, plane_out, plane_in, own, z_out, z_in,
        head_sem, m_send, m_recv, ici_send, core_send, g_recv, relay_send, relay_recv,
        st_send, st_recv, sz_send, sz_recv, c_send, c_recv, p_send, p_recv, z_send, z_recv,
    ) = scratch
    nc = n // 2
    me = lax.axis_index("dp")
    vi = lax.axis_index("vocab")
    core = lax.rem(me, 2)
    chip = lax.div(me, 2)
    partner = 2 * chip + 1 - core
    pair = 2 * rows
    width = n * pair
    ds, dt = shead.shape[0], thead.shape[0]

    head_copies = [
        pltpu.make_async_copy(shead_hbm, shead, head_sem.at[0]),
        pltpu.make_async_copy(thead_hbm, thead, head_sem.at[1]),
    ]
    for copy in head_copies:
        copy.start()

    barrier = pltpu.get_barrier_semaphore()
    for r in range(1, n):
        pl.semaphore_signal(barrier, inc=1, device_id={"dp": lax.rem(me + r, n)}, device_id_type=MESH)
    for r in range(1, nv):
        pl.semaphore_signal(barrier, inc=1, device_id={"vocab": lax.rem(vi + r, nv)}, device_id_type=MESH)

    def fold(i):
        b, at, size = cuts[i]
        ref = (sh_ref, th_ref)[b]
        half = ref.shape[1] // 2
        left = ref[:, at:at + size].astype(jnp.float32)
        right = ref[:, half + at:half + at + size].astype(jnp.float32)
        bufs[i][me] = jnp.concatenate([left, right], axis=0).astype(jnp.bfloat16)

    lane = lax.broadcasted_iota(jnp.int32, (1, width), 1)
    half_l = jnp.zeros((1, width), jnp.int32)
    shard_l = jnp.zeros((1, width), jnp.int32)
    pos_l = lane
    for i in range(1, 2 * n):
        pos_l = jnp.where(lane >= i * rows, lane - i * rows, pos_l)
        half_l = jnp.where(lane >= i * rows, i % 2, half_l)
        shard_l = jnp.where(lane >= i * rows, i // 2, shard_l)
    dest_l = jnp.zeros((1, width), jnp.int32)
    for i in range(rows):
        dest_l = jnp.where(pos_l == i, dest_ref[i], dest_l)
    here = shard_l == me
    gm[me] = jnp.concatenate(
        [
            jnp.where(here, live_ref[0], 0),
            jnp.where(shard_l > me, live_ref[0], 0),
            jnp.where(here, count_ref[0], 0),
            jnp.where(here, dest_l, 0),
            jnp.zeros((4, width), jnp.int32),
        ],
        axis=0,
    )
    fold(0)
    fold(1)
    pl.semaphore_wait(barrier, n - 1 + nv - 1)

    def remote(src, dst, send, recv, target):
        return pltpu.make_async_remote_copy(
            src_ref=src, dst_ref=dst, send_sem=send, recv_sem=recv,
            device_id=target, device_id_type=MESH,
        )

    waits = []

    late = []

    def go(copy, kept=waits):
        copy.start()
        kept.append(copy)

    square = nc == 4
    x_chip = 2 * lax.div(chip, 2) + 1 - lax.rem(chip, 2)
    y_chip = lax.rem(chip + 2, 4)
    targets = [x_chip, y_chip] if square else [lax.rem(chip + r, nc) for r in range(1, nc)]
    sources = [x_chip, y_chip] if square else [lax.rem(chip + nc - r, nc) for r in range(1, nc)]

    def block_copy(i, shard, send, target):
        return remote(bufs[i].at[shard], bufs[i].at[shard], send, g_recv.at[i, shard], {"dp": target})

    def start_own(i):
        for r, to in enumerate(targets):
            go(block_copy(i, me, ici_send.at[i, r], 2 * to + core))
        go(block_copy(i, me, core_send.at[i, 0], partner))

    def pass_on(i):
        for r, source in enumerate(sources):
            shard = 2 * source + core
            block_copy(i, shard, core_send.at[i, r + 1], partner).wait_recv()
            if square:
                size = bufs[i].shape[2] // 2
                to = (y_chip, x_chip)[r]
                part = bufs[i].at[shard, :, pl.ds(r * size, size)]
                go(remote(part, part, relay_send.at[i, r], relay_recv.at[i, r], {"dp": 2 * to + core}))
            go(block_copy(i, shard, core_send.at[i, r + 1], partner))

    def finish(i):
        if square:
            shard = 2 * (3 - chip) + core
            for r in range(2):
                size = bufs[i].shape[2] // 2
                part = bufs[i].at[shard, :, pl.ds(r * size, size)]
                remote(part, part, relay_send.at[i, r], relay_recv.at[i, r], {"dp": partner}).wait_recv()
            go(block_copy(i, shard, core_send.at[i, 3], partner))
        for c in range(nc):
            block_copy(i, 2 * c + 1 - core, core_send.at[i, 0], partner).wait_recv()

    for r in range(1, n):
        target = lax.rem(me + r, n)
        go(remote(gm.at[me], gm.at[me], m_send.at[r], m_recv.at[me], {"dp": target}))
    start_own(0)
    start_own(1)
    for i in range(2, npieces):
        fold(i)
    pass_on(0)
    start_own(2)
    for r in range(1, n):
        shard = lax.rem(me + r, n)
        remote(gm.at[shard], gm.at[shard], m_send.at[r], m_recv.at[shard], {"dp": shard}).wait_recv()
    meta = gm[0]
    for i in range(1, n):
        meta = meta + gm[i]
    live_l, off_l, count_l, dest_l = meta[0:1], meta[1:2], meta[2:3], meta[3:4]

    rank_l = jnp.zeros((1, width), jnp.int32)
    for i in range(n):
        off_i = off_l[:, i * pair:i * pair + 1]
        inside = (dest_l >= i * rows) & (dest_l < (i + 1) * rows)
        rank_l = jnp.where(inside, dest_l - i * rows + off_i, rank_l)
    shape = (2 * live, width)
    row = lax.broadcasted_iota(jnp.int32, shape, 0)
    key_s = jnp.where(pos_l < live_l, pos_l + off_l + live * half_l, -1)
    key_t = jnp.where(pos_l < count_l, rank_l + live * half_l, -1)
    onehot_s[...] = jnp.where(row == key_s, 1.0, 0.0).astype(jnp.bfloat16)
    onehot_t[...] = jnp.where(row == key_t, 1.0, 0.0).astype(jnp.bfloat16)

    def logits(i):
        b, at, size = cuts[i]
        onehot, head, out = ((onehot_s, shead, s_log), (onehot_t, thead, t_log))[b]
        half = head.shape[0] // 2
        packed = nn(onehot[...], bufs[i][...].reshape(width, size)).astype(jnp.bfloat16)
        top, low = packed[:live], packed[live:]
        if b == 0:
            hc_ref[:, at:at + size] = top
            hc_ref[:, half + at:half + at + size] = low
        value = nn(top, head[at:at + size, :]) + nn(low, head[half + at:half + at + size, :])
        out[...] = value if at == 0 else out[...] + value

    for i in range(npieces + 1):
        if 0 < i < npieces:
            pass_on(i)
            if i + 2 < npieces:
                start_own(i + 2)
        if i >= 1:
            finish(i - 1)
            b, at, _ = cuts[i - 1]
            if at == 0:
                head_copies[b].wait()
            logits(i - 1)

    lanes = st.shape[2]
    s_val, t_val = s_log[...], t_log[...]
    t_top = jnp.max(t_val, axis=1, keepdims=True)
    s_top = jnp.max(s_val, axis=1, keepdims=True)
    t_exp = jnp.exp(t_val - t_top)
    t_sum = jnp.sum(t_exp, axis=1, keepdims=True)
    s_sum = jnp.sum(jnp.exp(s_val - s_top), axis=1, keepdims=True)
    cross = jnp.sum(t_exp * (t_val - s_val), axis=1, keepdims=True)
    col = lax.broadcasted_iota(jnp.int32, (live, 128), 1)
    table = jnp.where(col == 0, t_top, 1.0)
    for i, value in ((1, s_top), (2, t_sum), (3, s_sum), (4, cross)):
        table = jnp.where(col == i, value, table)
    if lanes > live:
        table = jnp.concatenate([table, jnp.ones((lanes - live, 128), jnp.float32)], axis=0)
    st[me] = jnp.transpose(table)[0:8]
    for r in range(1, n):
        go(remote(st.at[me], st.at[me], st_send.at[r], st_recv.at[me], {"dp": lax.rem(me + r, n)}))
    tile = 512
    slabs = ds // tile

    def turn(first, last):
        for i in range(first, last):
            hct[i * tile:(i + 1) * tile, :] = jnp.transpose(hc_ref[:, i * tile:(i + 1) * tile])

    turn(0, slabs // 2)
    for r in range(1, n):
        shard = lax.rem(me + r, n)
        remote(st.at[shard], st.at[shard], st_send.at[r], st_recv.at[shard], {"dp": shard}).wait_recv()
    joined = merge(st, n)
    ones = jnp.ones((3, lanes), jnp.float32)
    sz[vi] = jnp.concatenate(list(joined) + [ones], axis=0)
    for r in range(1, nv):
        go(remote(sz.at[vi], sz.at[vi], sz_send.at[r], sz_recv.at[vi], {"vocab": lax.rem(vi + r, nv)}))
    turn(slabs // 2, slabs)
    for r in range(1, nv):
        shard = lax.rem(vi + r, nv)
        remote(sz.at[shard], sz.at[shard], sz_send.at[r], sz_recv.at[shard], {"vocab": shard}).wait_recv()
    t_top, s_top, t_sum, s_sum, cross = merge(sz, nv)
    t_norm = t_top + jnp.log(t_sum)
    s_norm = s_top + jnp.log(s_sum)
    divergence = cross / t_sum - t_norm + s_norm
    lane = lax.broadcasted_iota(jnp.int32, (1, lanes), 1)
    divergence = jnp.where(lane < live, divergence, 0.0)
    loss_ref[...] = jnp.sum(divergence, axis=1, keepdims=True) / live
    norms = jnp.concatenate([t_norm, s_norm, jnp.zeros((126, lanes), jnp.float32)], axis=0)
    norms = jnp.transpose(norms)[:live]
    gap = jnp.exp(s_val - norms[:, 1:2]) - jnp.exp(t_val - norms[:, 0:1])
    grad = (gap * (loss_scale / live)).astype(jnp.bfloat16)

    spread = tn(onehot_s[0:live, :], grad)
    sides = [
        jnp.concatenate([spread[(2 * c + k) * pair:(2 * c + k) * pair + rows] for c in range(nc)], axis=0)
        for k in range(2)
    ]
    is_zero = core == 0
    lgx[0:nc * rows] = jnp.where(is_zero, sides[1], sides[0]).astype(jnp.bfloat16)
    lgx[nc * rows:] = jnp.where(is_zero, sides[0], sides[1]).astype(jnp.bfloat16)

    half = core_out.shape[3]

    def partial(j):
        base = pl.multiple_of(lax.rem(vi + 1 + j, nv) * (2 * half), 16)
        low = nt(lgx[...], shead[pl.ds(base, half), :])
        high = nt(lgx[...], shead[pl.ds(pl.multiple_of(base + half, 16), half), :])
        blocks = [
            jnp.concatenate([low[c * rows:(c + 1) * rows], high[c * rows:(c + 1) * rows]], axis=0)
            for c in range(2 * nc)
        ]
        for c in range(nc):
            core_out[j, c] = blocks[c].astype(jnp.bfloat16)
        go(remote(core_out.at[j], core_in.at[j], c_send.at[j], c_recv.at[j], {"dp": partner}))
        for c in range(nc):
            mine[j, c] = blocks[nc + c]

    def to_plane(j):
        remote(core_out.at[j], core_in.at[j], c_send.at[j], c_recv.at[j], {"dp": partner}).wait_recv()
        mine[j] = mine[j] + core_in[j].astype(jnp.float32)
        plane_out[j] = mine[j].astype(jnp.bfloat16)
        for r in range(1, nc):
            to = lax.rem(chip + r, nc)
            go(remote(plane_out.at[j, to], plane_in.at[j, r], p_send.at[j, r], p_recv.at[j, r], {"dp": 2 * to + core}), late)

    for j in range(nv + 1):
        if j < nv:
            partial(j)
        if j >= 1:
            to_plane(j - 1)
    for j in range(nv):
        for i in range(slabs * j // nv, slabs * (j + 1) // nv):
            ghead_ref[i * tile:(i + 1) * tile, :] = nn(hct[i * tile:(i + 1) * tile, :], grad).astype(jnp.bfloat16)
        if j == 0:
            for copy in waits:
                copy.wait_send()
        total = mine[j, chip]
        for r in range(1, nc):
            remote(plane_in.at[j, r], plane_in.at[j, r], p_send.at[j, r], p_recv.at[j, r], {"dp": partner}).wait_recv()
            total = total + plane_in[j, r].astype(jnp.float32)
        if j < nv - 1:
            z_out[j] = total.astype(jnp.bfloat16)
            go(remote(z_out.at[j], z_in.at[j], z_send.at[j], z_recv.at[j], {"vocab": lax.rem(vi + 1 + j, nv)}), late)
        else:
            own[...] = total
    total = own[...]
    for j in range(nv - 1):
        remote(z_in.at[j], z_in.at[j], z_send.at[j], z_recv.at[j], {"vocab": lax.rem(vi + 1, nv)}).wait_recv()
        total = total + z_in[j].astype(jnp.float32)
    gh_ref[...] = jnp.concatenate([total[:rows], total[rows:]], axis=1).astype(jnp.bfloat16)
    for copy in late:
        copy.wait_send()


def per_device(
    student_hidden,
    teacher_hidden,
    student_head,
    teacher_head,
    live_count,
    teacher_count,
    teacher_dest,
):
    rows, ds = student_hidden.shape
    dt = teacher_hidden.shape[1]
    vocab = student_head.shape[1]
    n = lax.axis_size("dp")
    nv = lax.axis_size("vocab")
    nc = n // 2
    live = rows * n // 2
    lanes = -(-live // 128) * 128
    pair = 2 * rows
    width = n * pair
    half = ds // nv // 2
    bf16, f32 = jnp.bfloat16, jnp.float32
    vmem = pl.BlockSpec(memory_space=pltpu.VMEM)
    hbm = pl.BlockSpec(memory_space=pltpu.HBM)
    dma = pltpu.SemaphoreType.DMA
    smem = pl.BlockSpec(memory_space=pltpu.SMEM)
    cuts = []
    for b, sizes in enumerate(((1792,), (1280, 1024))):
        at = 0
        for size in sizes:
            cuts.append((b, at, size))
            at += size
        assert at == (ds, dt)[b] // 2
    pieces = len(cuts)
    loss, grad_head, grad_hidden = pl.pallas_call(
        functools.partial(main_kernel, n, nv, rows, live, cuts, pieces),
        out_shape=(
            jax.ShapeDtypeStruct((1, 1), f32),
            pltpu.VMEM((ds, vocab), bf16),
            pltpu.VMEM((rows, 2 * half), bf16),
        ),
        in_specs=[vmem, vmem, smem, smem, smem, hbm, hbm],
        out_specs=(vmem, vmem, vmem),
        scratch_shapes=[
            *[pltpu.VMEM((n, pair, size), bf16) for _, _, size in cuts],
            pltpu.VMEM((n, 8, width), jnp.int32),
            pltpu.VMEM((ds, vocab), bf16),
            pltpu.VMEM((dt, vocab), bf16),
            pltpu.VMEM((2 * live, width), bf16),
            pltpu.VMEM((2 * live, width), bf16),
            pltpu.VMEM((live, ds), bf16),
            pltpu.VMEM((ds, live), bf16),
            pltpu.VMEM((live, vocab), f32),
            pltpu.VMEM((live, vocab), f32),
            pltpu.VMEM((n, 8, lanes), f32),
            pltpu.VMEM((nv, 8, lanes), f32),
            pltpu.VMEM((2 * nc * rows, vocab), bf16),
            pltpu.VMEM((nv, nc, pair, half), bf16),
            pltpu.VMEM((nv, nc, pair, half), bf16),
            pltpu.VMEM((nv, nc, pair, half), f32),
            pltpu.VMEM((nv, nc, pair, half), bf16),
            pltpu.VMEM((nv, nc, pair, half), bf16),
            pltpu.VMEM((pair, half), f32),
            pltpu.VMEM((nv, pair, half), bf16),
            pltpu.VMEM((nv, pair, half), bf16),
            dma((2,)),
            dma((n,)), dma((n,)),
            dma((pieces, nc)), dma((pieces, nc)), dma((pieces, n)), dma((pieces, 2)), dma((pieces, 2)),
            dma((n,)), dma((n,)), dma((nv,)), dma((nv,)),
            dma((nv,)), dma((nv,)), dma((nv, nc)), dma((nv, nc)), dma((nv,)), dma((nv,)),
        ],
        compiler_params=pltpu.CompilerParams(
            collective_id=0, has_side_effects=True, vmem_limit_bytes=(56 if n <= 8 else 58) * 2**20
        ),
        name="distill",
    )(student_hidden, teacher_hidden, live_count, teacher_count, teacher_dest, student_head, teacher_head)
    return (loss[0, 0], grad_hidden, grad_head)


def solution(mesh):
    return jax.shard_map(
        per_device,
        mesh=mesh,
        in_specs=(
            P("dp", None),
            P("dp", None),
            P(None, ("dp", "vocab")),
            P(None, ("dp", "vocab")),
            P("dp"),
            P("dp"),
            P("dp"),
        ),
        out_specs=(P(), P("dp", "vocab"), P(None, ("dp", "vocab"))),
        check_vma=False,
    )
```

```python
import functools

import jax
import jax.numpy as jnp
from jax import lax
from jax.experimental import pallas as pl
from jax.experimental.pallas import tpu as pltpu
from jax.sharding import PartitionSpec as P

loss_scale = 65536.0
MESH = pl.DeviceIdType.MESH


def nt(a, b):
    return lax.dot_general(a, b, (((1,), (1,)), ((), ())), preferred_element_type=jnp.float32)


def tn(a, b):
    return lax.dot_general(a, b, (((0,), (0,)), ((), ())), preferred_element_type=jnp.float32)


def nn(a, b):
    return jnp.dot(a, b, preferred_element_type=jnp.float32)


def merge(parts, count):
    t_top = parts[0, 0:1]
    s_top = parts[0, 1:2]
    for i in range(1, count):
        t_top = jnp.maximum(t_top, parts[i, 0:1])
        s_top = jnp.maximum(s_top, parts[i, 1:2])
    t_sum = jnp.zeros_like(t_top)
    s_sum = jnp.zeros_like(t_top)
    cross = jnp.zeros_like(t_top)
    for i in range(count):
        t_scale = jnp.exp(parts[i, 0:1] - t_top)
        t_sum += parts[i, 2:3] * t_scale
        cross += parts[i, 4:5] * t_scale
        s_sum += parts[i, 3:4] * jnp.exp(parts[i, 1:2] - s_top)
    return t_top, s_top, t_sum, s_sum, cross


def main_kernel(
    n, nv, rows, live, cuts, npieces,
    sh_ref, th_ref, live_ref, count_ref, dest_ref, shead_hbm, thead_hbm,
    loss_ref, ghead_ref, gh_ref, *scratch,
):
    bufs, scratch = scratch[:npieces], scratch[npieces:]
    (
        gm, shead, thead, onehot_s, onehot_t, hc_ref, hct, s_log, t_log,
        st, sz, lgx, core_out, core_in, mine, plane_out, plane_in, own, z_out, z_in,
        head_sem, m_send, m_recv, ici_send, core_send, g_recv, relay_send, relay_recv,
        st_send, st_recv, sz_send, sz_recv, c_send, c_recv, p_send, p_recv, z_send, z_recv,
    ) = scratch
    nc = n // 2
    me = lax.axis_index("dp")
    vi = lax.axis_index("vocab")
    core = lax.rem(me, 2)
    chip = lax.div(me, 2)
    partner = 2 * chip + 1 - core
    pair = 2 * rows
    width = n * pair
    ds, dt = shead.shape[0], thead.shape[0]

    head_copies = [
        pltpu.make_async_copy(shead_hbm, shead, head_sem.at[0]),
        pltpu.make_async_copy(thead_hbm, thead, head_sem.at[1]),
    ]
    for copy in head_copies:
        copy.start()

    barrier = pltpu.get_barrier_semaphore()
    for r in range(1, n):
        pl.semaphore_signal(barrier, inc=1, device_id={"dp": lax.rem(me + r, n)}, device_id_type=MESH)
    for r in range(1, nv):
        pl.semaphore_signal(barrier, inc=1, device_id={"vocab": lax.rem(vi + r, nv)}, device_id_type=MESH)

    def fold(i):
        b, at, size = cuts[i]
        ref = (sh_ref, th_ref)[b]
        half = ref.shape[1] // 2
        left = ref[:, at:at + size].astype(jnp.float32)
        right = ref[:, half + at:half + at + size].astype(jnp.float32)
        bufs[i][me] = jnp.concatenate([left, right], axis=0).astype(jnp.bfloat16)

    lane = lax.broadcasted_iota(jnp.int32, (1, width), 1)
    half_l = jnp.zeros((1, width), jnp.int32)
    shard_l = jnp.zeros((1, width), jnp.int32)
    pos_l = lane
    for i in range(1, 2 * n):
        pos_l = jnp.where(lane >= i * rows, lane - i * rows, pos_l)
        half_l = jnp.where(lane >= i * rows, i % 2, half_l)
        shard_l = jnp.where(lane >= i * rows, i // 2, shard_l)
    dest_l = jnp.zeros((1, width), jnp.int32)
    for i in range(rows):
        dest_l = jnp.where(pos_l == i, dest_ref[i], dest_l)
    here = shard_l == me
    gm[me] = jnp.concatenate(
        [
            jnp.where(here, live_ref[0], 0),
            jnp.where(shard_l > me, live_ref[0], 0),
            jnp.where(here, count_ref[0], 0),
            jnp.where(here, dest_l, 0),
            jnp.zeros((4, width), jnp.int32),
        ],
        axis=0,
    )
    fold(0)
    fold(1)
    pl.semaphore_wait(barrier, n - 1 + nv - 1)

    def remote(src, dst, send, recv, target):
        return pltpu.make_async_remote_copy(
            src_ref=src, dst_ref=dst, send_sem=send, recv_sem=recv,
            device_id=target, device_id_type=MESH,
        )

    waits = []

    late = []

    def go(copy, kept=waits):
        copy.start()
        kept.append(copy)

    square = nc == 4
    x_chip = 2 * lax.div(chip, 2) + 1 - lax.rem(chip, 2)
    y_chip = lax.rem(chip + 2, 4)
    targets = [x_chip, y_chip] if square else [lax.rem(chip + r, nc) for r in range(1, nc)]
    sources = [x_chip, y_chip] if square else [lax.rem(chip + nc - r, nc) for r in range(1, nc)]

    def block_copy(i, shard, send, target):
        return remote(bufs[i].at[shard], bufs[i].at[shard], send, g_recv.at[i, shard], {"dp": target})

    def start_own(i):
        for r, to in enumerate(targets):
            go(block_copy(i, me, ici_send.at[i, r], 2 * to + core))
        go(block_copy(i, me, core_send.at[i, 0], partner))

    def pass_on(i):
        for r, source in enumerate(sources):
            shard = 2 * source + core
            block_copy(i, shard, core_send.at[i, r + 1], partner).wait_recv()
            if square:
                size = bufs[i].shape[2] // 2
                to = (y_chip, x_chip)[r]
                part = bufs[i].at[shard, :, pl.ds(r * size, size)]
                go(remote(part, part, relay_send.at[i, r], relay_recv.at[i, r], {"dp": 2 * to + core}))
            go(block_copy(i, shard, core_send.at[i, r + 1], partner))

    def finish(i):
        if square:
            shard = 2 * (3 - chip) + core
            for r in range(2):
                size = bufs[i].shape[2] // 2
                part = bufs[i].at[shard, :, pl.ds(r * size, size)]
                remote(part, part, relay_send.at[i, r], relay_recv.at[i, r], {"dp": partner}).wait_recv()
            go(block_copy(i, shard, core_send.at[i, 3], partner))
        for c in range(nc):
            block_copy(i, 2 * c + 1 - core, core_send.at[i, 0], partner).wait_recv()

    for r in range(1, n):
        target = lax.rem(me + r, n)
        go(remote(gm.at[me], gm.at[me], m_send.at[r], m_recv.at[me], {"dp": target}))
    start_own(0)
    start_own(1)
    for i in range(2, npieces):
        fold(i)
    pass_on(0)
    start_own(2)
    for r in range(1, n):
        shard = lax.rem(me + r, n)
        remote(gm.at[shard], gm.at[shard], m_send.at[r], m_recv.at[shard], {"dp": shard}).wait_recv()
    meta = gm[0]
    for i in range(1, n):
        meta = meta + gm[i]
    live_l, off_l, count_l, dest_l = meta[0:1], meta[1:2], meta[2:3], meta[3:4]

    rank_l = jnp.zeros((1, width), jnp.int32)
    for i in range(n):
        off_i = off_l[:, i * pair:i * pair + 1]
        inside = (dest_l >= i * rows) & (dest_l < (i + 1) * rows)
        rank_l = jnp.where(inside, dest_l - i * rows + off_i, rank_l)
    shape = (2 * live, width)
    row = lax.broadcasted_iota(jnp.int32, shape, 0)
    key_s = jnp.where(pos_l < live_l, pos_l + off_l + live * half_l, -1)
    key_t = jnp.where(pos_l < count_l, rank_l + live * half_l, -1)
    onehot_s[...] = jnp.where(row == key_s, 1.0, 0.0).astype(jnp.bfloat16)
    onehot_t[...] = jnp.where(row == key_t, 1.0, 0.0).astype(jnp.bfloat16)

    def logits(i):
        b, at, size = cuts[i]
        onehot, head, out = ((onehot_s, shead, s_log), (onehot_t, thead, t_log))[b]
        half = head.shape[0] // 2
        packed = nn(onehot[...], bufs[i][...].reshape(width, size)).astype(jnp.bfloat16)
        top, low = packed[:live], packed[live:]
        if b == 0:
            hc_ref[:, at:at + size] = top
            hc_ref[:, half + at:half + at + size] = low
        value = nn(top, head[at:at + size, :]) + nn(low, head[half + at:half + at + size, :])
        out[...] = value if at == 0 else out[...] + value

    for i in range(npieces + 1):
        if 0 < i < npieces:
            pass_on(i)
            if i + 2 < npieces:
                start_own(i + 2)
        if i >= 1:
            finish(i - 1)
            b, at, _ = cuts[i - 1]
            if at == 0:
                head_copies[b].wait()
            logits(i - 1)

    lanes = st.shape[2]
    s_val, t_val = s_log[...], t_log[...]
    t_top = jnp.max(t_val, axis=1, keepdims=True)
    s_top = jnp.max(s_val, axis=1, keepdims=True)
    t_exp = jnp.exp(t_val - t_top)
    t_sum = jnp.sum(t_exp, axis=1, keepdims=True)
    s_sum = jnp.sum(jnp.exp(s_val - s_top), axis=1, keepdims=True)
    cross = jnp.sum(t_exp * (t_val - s_val), axis=1, keepdims=True)
    col = lax.broadcasted_iota(jnp.int32, (live, 128), 1)
    table = jnp.where(col == 0, t_top, 1.0)
    for i, value in ((1, s_top), (2, t_sum), (3, s_sum), (4, cross)):
        table = jnp.where(col == i, value, table)
    if lanes > live:
        table = jnp.concatenate([table, jnp.ones((lanes - live, 128), jnp.float32)], axis=0)
    st[me] = jnp.transpose(table)[0:8]
    for r in range(1, n):
        go(remote(st.at[me], st.at[me], st_send.at[r], st_recv.at[me], {"dp": lax.rem(me + r, n)}))
    tile = 512
    slabs = ds // tile

    def turn(first, last):
        for i in range(first, last):
            hct[i * tile:(i + 1) * tile, :] = jnp.transpose(hc_ref[:, i * tile:(i + 1) * tile])

    turn(0, slabs // 2)
    for r in range(1, n):
        shard = lax.rem(me + r, n)
        remote(st.at[shard], st.at[shard], st_send.at[r], st_recv.at[shard], {"dp": shard}).wait_recv()
    joined = merge(st, n)
    ones = jnp.ones((3, lanes), jnp.float32)
    sz[vi] = jnp.concatenate(list(joined) + [ones], axis=0)
    for r in range(1, nv):
        go(remote(sz.at[vi], sz.at[vi], sz_send.at[r], sz_recv.at[vi], {"vocab": lax.rem(vi + r, nv)}))
    turn(slabs // 2, slabs)
    for r in range(1, nv):
        shard = lax.rem(vi + r, nv)
        remote(sz.at[shard], sz.at[shard], sz_send.at[r], sz_recv.at[shard], {"vocab": shard}).wait_recv()
    t_top, s_top, t_sum, s_sum, cross = merge(sz, nv)
    t_norm = t_top + jnp.log(t_sum)
    s_norm = s_top + jnp.log(s_sum)
    divergence = cross / t_sum - t_norm + s_norm
    lane = lax.broadcasted_iota(jnp.int32, (1, lanes), 1)
    divergence = jnp.where(lane < live, divergence, 0.0)
    loss_ref[...] = jnp.sum(divergence, axis=1, keepdims=True) / live
    norms = jnp.concatenate([t_norm, s_norm, jnp.zeros((126, lanes), jnp.float32)], axis=0)
    norms = jnp.transpose(norms)[:live]
    gap = jnp.exp(s_val - norms[:, 1:2]) - jnp.exp(t_val - norms[:, 0:1])
    grad = (gap * (loss_scale / live)).astype(jnp.bfloat16)

    spread = tn(onehot_s[0:live, :], grad)
    sides = [
        jnp.concatenate([spread[(2 * c + k) * pair:(2 * c + k) * pair + rows] for c in range(nc)], axis=0)
        for k in range(2)
    ]
    is_zero = core == 0
    lgx[0:nc * rows] = jnp.where(is_zero, sides[1], sides[0]).astype(jnp.bfloat16)
    lgx[nc * rows:] = jnp.where(is_zero, sides[0], sides[1]).astype(jnp.bfloat16)

    half = core_out.shape[3]

    def partial(j):
        base = pl.multiple_of(lax.rem(vi + 1 + j, nv) * (2 * half), 16)
        low = nt(lgx[...], shead[pl.ds(base, half), :])
        high = nt(lgx[...], shead[pl.ds(pl.multiple_of(base + half, 16), half), :])
        blocks = [
            jnp.concatenate([low[c * rows:(c + 1) * rows], high[c * rows:(c + 1) * rows]], axis=0)
            for c in range(2 * nc)
        ]
        for c in range(nc):
            core_out[j, c] = blocks[c].astype(jnp.bfloat16)
        for c in range(nc):
            mine[j, c] = blocks[nc + c]

    group = nv // 2 if nv % 2 == 0 else nv

    def cross_core(first):
        at = pl.ds(first, group)
        return remote(core_out.at[at], core_in.at[at], c_send.at[first], c_recv.at[first], {"dp": partner})

    def plane(first, r, to):
        at = pl.ds(first, group)
        return remote(
            plane_out.at[at, to], plane_in.at[at, r], p_send.at[first, r], p_recv.at[first, r], {"dp": 2 * to + core}
        )

    def to_plane(first):
        cross_core(first).wait_recv()
        at = pl.ds(first, group)
        mine[at] = mine[at] + core_in[at].astype(jnp.float32)
        plane_out[at] = mine[at].astype(jnp.bfloat16)
        for r in range(1, nc):
            go(plane(first, r, lax.rem(chip + r, nc)), late)

    for first in range(0, nv + group, group):
        if first < nv:
            for j in range(first, first + group):
                partial(j)
            go(cross_core(first))
        if first >= group:
            to_plane(first - group)
    for j in range(nv):
        for i in range(slabs * j // nv, slabs * (j + 1) // nv):
            ghead_ref[i * tile:(i + 1) * tile, :] = nn(hct[i * tile:(i + 1) * tile, :], grad).astype(jnp.bfloat16)
        if j == 0:
            for copy in waits:
                copy.wait_send()
        total = mine[j, chip]
        for r in range(1, nc):
            if j % group == 0:
                plane(j, r, lax.rem(chip + r, nc)).wait_recv()
            total = total + plane_in[j, r].astype(jnp.float32)
        if j < nv - 1:
            z_out[j] = total.astype(jnp.bfloat16)
            go(remote(z_out.at[j], z_in.at[j], z_send.at[j], z_recv.at[j], {"vocab": lax.rem(vi + 1 + j, nv)}), late)
        else:
            own[...] = total
    total = own[...]
    for j in range(nv - 1):
        remote(z_in.at[j], z_in.at[j], z_send.at[j], z_recv.at[j], {"vocab": lax.rem(vi + 1, nv)}).wait_recv()
        total = total + z_in[j].astype(jnp.float32)
    gh_ref[...] = jnp.concatenate([total[:rows], total[rows:]], axis=1).astype(jnp.bfloat16)
    for copy in late:
        copy.wait_send()


def per_device(
    student_hidden,
    teacher_hidden,
    student_head,
    teacher_head,
    live_count,
    teacher_count,
    teacher_dest,
):
    rows, ds = student_hidden.shape
    dt = teacher_hidden.shape[1]
    vocab = student_head.shape[1]
    n = lax.axis_size("dp")
    nv = lax.axis_size("vocab")
    nc = n // 2
    live = rows * n // 2
    lanes = -(-live // 128) * 128
    pair = 2 * rows
    width = n * pair
    half = ds // nv // 2
    bf16, f32 = jnp.bfloat16, jnp.float32
    vmem = pl.BlockSpec(memory_space=pltpu.VMEM)
    hbm = pl.BlockSpec(memory_space=pltpu.HBM)
    dma = pltpu.SemaphoreType.DMA
    smem = pl.BlockSpec(memory_space=pltpu.SMEM)
    cuts = []
    for b, sizes in enumerate(((1792,), (1280, 1024))):
        at = 0
        for size in sizes:
            cuts.append((b, at, size))
            at += size
        assert at == (ds, dt)[b] // 2
    pieces = len(cuts)
    loss, grad_head, grad_hidden = pl.pallas_call(
        functools.partial(main_kernel, n, nv, rows, live, cuts, pieces),
        out_shape=(
            jax.ShapeDtypeStruct((1, 1), f32),
            pltpu.VMEM((ds, vocab), bf16),
            pltpu.VMEM((rows, 2 * half), bf16),
        ),
        in_specs=[vmem, vmem, smem, smem, smem, hbm, hbm],
        out_specs=(vmem, vmem, vmem),
        scratch_shapes=[
            *[pltpu.VMEM((n, pair, size), bf16) for _, _, size in cuts],
            pltpu.VMEM((n, 8, width), jnp.int32),
            pltpu.VMEM((ds, vocab), bf16),
            pltpu.VMEM((dt, vocab), bf16),
            pltpu.VMEM((2 * live, width), bf16),
            pltpu.VMEM((2 * live, width), bf16),
            pltpu.VMEM((live, ds), bf16),
            pltpu.VMEM((ds, live), bf16),
            pltpu.VMEM((live, vocab), f32),
            pltpu.VMEM((live, vocab), f32),
            pltpu.VMEM((n, 8, lanes), f32),
            pltpu.VMEM((nv, 8, lanes), f32),
            pltpu.VMEM((2 * nc * rows, vocab), bf16),
            pltpu.VMEM((nv, nc, pair, half), bf16),
            pltpu.VMEM((nv, nc, pair, half), bf16),
            pltpu.VMEM((nv, nc, pair, half), f32),
            pltpu.VMEM((nv, nc, pair, half), bf16),
            pltpu.VMEM((nv, nc, pair, half), bf16),
            pltpu.VMEM((pair, half), f32),
            pltpu.VMEM((nv, pair, half), bf16),
            pltpu.VMEM((nv, pair, half), bf16),
            dma((2,)),
            dma((n,)), dma((n,)),
            dma((pieces, nc)), dma((pieces, nc)), dma((pieces, n)), dma((pieces, 2)), dma((pieces, 2)),
            dma((n,)), dma((n,)), dma((nv,)), dma((nv,)),
            dma((nv,)), dma((nv,)), dma((nv, nc)), dma((nv, nc)), dma((nv,)), dma((nv,)),
        ],
        compiler_params=pltpu.CompilerParams(
            collective_id=0, has_side_effects=True, vmem_limit_bytes=(56 if n <= 8 else 58) * 2**20
        ),
        name="distill",
    )(student_hidden, teacher_hidden, live_count, teacher_count, teacher_dest, student_head, teacher_head)
    return (loss[0, 0], grad_hidden, grad_head)


def solution(mesh):
    return jax.shard_map(
        per_device,
        mesh=mesh,
        in_specs=(
            P("dp", None),
            P("dp", None),
            P(None, ("dp", "vocab")),
            P(None, ("dp", "vocab")),
            P("dp"),
            P("dp"),
            P("dp"),
        ),
        out_specs=(P(), P("dp", "vocab"), P(None, ("dp", "vocab"))),
        check_vma=False,
    )
```
